128 devices in a mesh: grp: 16 (over z, x_lo, core), sp: 8 (over x_hi, y).
Axes of the slice: x: 4 (x_hi: 2, x_lo: 2; x = x_hi * 2 + x_lo), y: 4, z: 4, core: 2. Of those that a mesh axis runs over, the one named last changes fastest.
Arguments:
- hidden_in: bfloat16 [16, 1024, 4096], P('grp', 'sp'), may hold values from -6 to 6
- queries: bfloat16 [16, 1024, 4096], P('grp', 'sp'), may hold values from -5 to 5
- key_heads: bfloat16 [16, 1024, 1024], P('grp', 'sp'), may hold values from -5 to 5
- saved_value_heads: bfloat16 [16, 1024, 1024], P('grp', 'sp'), may hold values from -6 to 6
- out_grads: bfloat16 [16, 1024, 4096], P('grp', 'sp'), may hold values from -24 to 24
- doc_ids: int32 [16, 1024], P('grp', 'sp'), may hold values from 0 to 2, never falling along the last dimension, each value on 1 to 512 neighbouring positions
Outputs:
- query_weight_grad: float32 [4096, 4096], P('grp', 'sp')
- key_weight_grad: float32 [4096, 1024], P('grp', 'sp')
- value_weight_grad: float32 [4096, 1024], P('grp', 'sp')
The draws below stay inside these ranges and needn't reach their ends.
Inputs may be any that keep to these rules, and one draw needn't show every extreme that they name: `doc_ids`: within each group's 1024 tokens the ids never fall; a document holds 1 to 512 tokens.
All inputs are finite; a program needn't handle non-finite values.
Results may differ from the reference program's by a relative error of at most 0.011.
Values may be sent and summed in bfloat16 or wider, within the bound.
No kernel may reach another device: no remote copies, remote signals or barrier semaphores. Data moves between devices by JAX's collectives and lax.ppermute only.
A program may use at most 128 MiB of HBM per device.

```python
import math
import jax
import jax.numpy as jnp
import numpy as np
from jax import lax

D = 4096
QUERY_HEADS = 32
KEY_VALUE_HEADS = 8
HEAD_SIZE = 128
GROUP_TOKENS = 1024
DOC_GROUP_COUNT = 16
TOKENS = 16384


def draw_key_heads(key, part):
    key = jax.random.fold_in(key, 7)
    array_shape = (DOC_GROUP_COUNT, GROUP_TOKENS, KEY_VALUE_HEADS * HEAD_SIZE)
    base = jnp.clip(jax.random.normal(key, array_shape, jnp.float32), -5.0, 5.0)
    return base.astype(jnp.bfloat16)


def draw_queries(key, part):
    key = jax.random.fold_in(key, 8)
    array_shape = (DOC_GROUP_COUNT, GROUP_TOKENS, QUERY_HEADS * HEAD_SIZE)
    base = jnp.clip(jax.random.normal(key, array_shape, jnp.float32), -5.0, 5.0)
    return base.astype(jnp.bfloat16)


def spiked(entries, own_key, source, target, blocks, factor):
    owner, partner = [(jnp.arange(entries.shape[position]) // (entries.shape[position] // blocks)).reshape([-1 if axis == position else 1 for axis in range(entries.ndim)]) for position in (source, target)]
    chosen = jax.random.permutation(own_key, blocks)[partner]
    strong = (owner == chosen) | (owner == (partner + blocks // 2) % blocks)
    return jnp.where(strong, factor * entries, entries)


def steps_of(stream_key, shape, split, least, largest):
    factor_of, own = 1.0, jax.random.fold_in(stream_key, 6)
    for dim, blocks in split:
        heights = jnp.exp(jax.random.uniform(jax.random.fold_in(own, dim), (blocks,), jnp.float32, least / len(split), largest / len(split)))
        factor_of = factor_of * jnp.repeat(heights, shape[dim] // blocks).reshape([-1 if axis == dim else 1 for axis in range(len(shape))])
    return factor_of


def length_profile(count, total, bound, skew):
    loads = [(1 << 20) // math.isqrt(standing ** skew) + 1 for standing in range(2, count + 1)]
    spare, holding = total - bound - (count - 1), [1] * (count - 1)
    while spare > 0:
        candidates = [i for i in range(count - 1) if holding[i] < bound]
        whole, remaining = sum([loads[i] for i in candidates]), spare
        for i in candidates:
            more = min(bound - holding[i], max(1, remaining * loads[i] // whole), spare)
            holding[i] = holding[i] + more
            spare = spare - more
    return np.array([bound] + holding)


def uneven(rng, amount, total, reach, skew):
    if amount == 2:
        one = jax.random.randint(rng, (), max(1, total - reach), min(reach, total - 1) + 1)
        return jnp.stack([one, total - one])
    tallies = jnp.asarray(length_profile(amount, total, reach, skew), jnp.int32)
    couples = (amount - 1) // 2
    donor, taker = tallies[1:1 + 2 * couples:2], tallies[2:2 + 2 * couples:2]
    room = jnp.minimum(donor - 1, reach - taker)
    passed = jax.random.randint(jax.random.fold_in(rng, 1), (couples,), 0, 1 << 20) % (room + 1)
    tallies = tallies.at[1:1 + 2 * couples:2].set(donor - passed).at[2:2 + 2 * couples:2].set(taker + passed)
    return tallies[jax.random.permutation(jax.random.fold_in(rng, 2), amount)]


def centred(own_key, extent, width, reach, cuts=(), dtype=jnp.bfloat16):
    result = width * jax.random.normal(own_key, extent, jnp.float32)
    if cuts:
        result = result * steps_of(own_key, extent, cuts, -0.22, 0.18)
    return jnp.clip(result, -reach, reach).astype(dtype)


def heavy_noise(own_key, dims, spread, reach, cuts, heavy, kind=jnp.bfloat16):
    values = spread * jax.random.normal(own_key, dims, jnp.float32)
    if cuts:
        values = values * steps_of(own_key, dims, cuts, -0.22, 0.18)
    return jnp.clip(spiked(values, jax.random.fold_in(own_key, 3), *heavy), -reach, reach).astype(kind)


def setup_inputs(seed: int = 0) -> dict:
    key_of = jax.random.split(jax.random.key(seed), 7)
    return {
        "hidden_in": heavy_noise(key_of[0], (DOC_GROUP_COUNT, GROUP_TOKENS, D), 1.0, 6.0, ((0, 16), (1, 8)), (0, 2, 16, 2.0)),
        "queries": draw_queries(jax.random.fold_in(key_of[6], 71), 0),
        "key_heads": draw_key_heads(jax.random.fold_in(key_of[6], 71), 0),
        "saved_value_heads": centred(key_of[3], (DOC_GROUP_COUNT, GROUP_TOKENS, KEY_VALUE_HEADS * HEAD_SIZE), 1.0, 6.0, ((0, 16), (1, 8))),
        "out_grads": centred(key_of[4], (DOC_GROUP_COUNT, GROUP_TOKENS, QUERY_HEADS * HEAD_SIZE), 4.0, 24.0, ((0, 16), (1, 8))),
        "doc_ids": jax.vmap(lambda own: jnp.searchsorted(jnp.cumsum(uneven(own, 3, GROUP_TOKENS, GROUP_TOKENS // 2, 2)), jnp.arange(GROUP_TOKENS), side="right"))(jax.random.split(key_of[5], DOC_GROUP_COUNT)).reshape((DOC_GROUP_COUNT, GROUP_TOKENS)).astype(jnp.int32),
    }


NEG = -1e+30

def one_kv_head(query_part, key_part, value_part, grad_part, allowed):
    score_scale = 1.0 / HEAD_SIZE ** 0.5
    queries_f = query_part.astype(jnp.float32)
    keys_f = key_part.astype(jnp.float32)
    values_f = value_part.astype(jnp.float32)
    grads_f = grad_part.astype(jnp.float32)
    scores = jnp.einsum('qgd,sd->gqs', queries_f, keys_f) * score_scale
    scores = jnp.where(allowed[None], scores, NEG)
    top = lax.optimization_barrier(jnp.max(scores, axis=-1, keepdims=True))
    log_total = top + jnp.log(lax.optimization_barrier(jnp.sum(jnp.exp(scores - top), axis=-1, keepdims=True)))
    probs = jnp.exp(scores - log_total)
    probs_low = lax.optimization_barrier(probs.astype(jnp.bfloat16)).astype(jnp.float32)
    attended = jnp.einsum('gqs,sd->qgd', probs_low, values_f)
    row_delta = lax.optimization_barrier(jnp.sum(grads_f * attended, axis=-1))
    prob_grads = jnp.einsum('qgd,sd->gqs', grads_f, values_f)
    score_grads = probs * (prob_grads - row_delta.T[:, :, None]) * score_scale
    score_low = lax.optimization_barrier(score_grads.astype(jnp.bfloat16)).astype(jnp.float32)
    query_grad = jnp.einsum('gqs,sd->qgd', score_low, keys_f).astype(jnp.bfloat16)
    key_gradient = jnp.einsum('gqs,qgd->sd', score_low, queries_f).astype(jnp.bfloat16)
    value_gradient = jnp.einsum('gqs,qgd->sd', probs_low, grads_f).astype(jnp.bfloat16)
    return (query_grad, key_gradient, value_gradient)

def one_group(operands):
    query_row_set, key_row_set, value_row_set, gradient_row_set, seg_row = operands
    group_extent = QUERY_HEADS // KEY_VALUE_HEADS
    positions = jnp.arange(GROUP_TOKENS)
    allowed = (positions[None, :] <= positions[:, None]) & (seg_row[None, :] == seg_row[:, None])
    query_pieces = query_row_set.reshape(GROUP_TOKENS, KEY_VALUE_HEADS, group_extent, HEAD_SIZE).transpose(1, 0, 2, 3)
    gradient_pieces = gradient_row_set.reshape(GROUP_TOKENS, KEY_VALUE_HEADS, group_extent, HEAD_SIZE).transpose(1, 0, 2, 3)
    key_pieces = key_row_set.reshape(GROUP_TOKENS, KEY_VALUE_HEADS, HEAD_SIZE).transpose(1, 0, 2)
    value_pieces = value_row_set.reshape(GROUP_TOKENS, KEY_VALUE_HEADS, HEAD_SIZE).transpose(1, 0, 2)

    def per_head(items):
        return one_kv_head(items[0], items[1], items[2], items[3], allowed)
    final_results = lax.map(per_head, (query_pieces, key_pieces, value_pieces, gradient_pieces))
    query_grad = final_results[0].transpose(1, 0, 2, 3).reshape(GROUP_TOKENS, QUERY_HEADS * HEAD_SIZE)
    key_gradient = final_results[1].transpose(1, 0, 2).reshape(GROUP_TOKENS, KEY_VALUE_HEADS * HEAD_SIZE)
    value_gradient = final_results[2].transpose(1, 0, 2).reshape(GROUP_TOKENS, KEY_VALUE_HEADS * HEAD_SIZE)
    return (query_grad, key_gradient, value_gradient)

def reference(hidden_in, queries, key_heads, saved_value_heads, out_grads, doc_ids):
    query_grads, key_grads, value_grads = lax.map(one_group, (queries, key_heads, saved_value_heads, out_grads, doc_ids))
    flat_in = hidden_in.reshape(-1, D)
    factor = TOKENS ** (-0.5)

    def weight_grad(grads):
        flat_grads = grads.reshape(flat_in.shape[0], -1)
        return jnp.dot(flat_in.T, flat_grads, preferred_element_type=jnp.float32) * factor
    return (weight_grad(query_grads), weight_grad(key_grads), weight_grad(value_grads))
```

```python
import math

import jax
import jax.numpy as jnp
from jax import lax
from jax.experimental import pallas as pl
from jax.experimental.pallas import tpu as pltpu
from jax.sharding import PartitionSpec as P

HEAD = 128
NEG = -1e30
SCALE = 1.0 / math.sqrt(HEAD)
FACTOR = 16384 ** -0.5
NJ = 1
BW = 256 // NJ
VM = 60 * 1024 * 1024
F32 = jnp.float32
BF16 = jnp.bfloat16
ANY = pl.BlockSpec(memory_space=pl.ANY)
VMEM = pl.BlockSpec(memory_space=pltpu.VMEM)


def place():
    g = lax.axis_index("grp")
    s = lax.axis_index("sp")
    return dict(
        z=g // 4, x=(s // 4) * 2 + (g // 2) % 2, c=lax.rem(g, 2), y=lax.rem(s, 4), xh=s // 4
    )


def pairs(dx=0, dy=0, dz=0, dc=0, only_half=None):
    out = []
    for z in range(4):
        for x in range(4):
            for y in range(4):
                for c in range(2):
                    if only_half is not None and x // 2 != only_half:
                        continue

                    def flat(z, x, y, c):
                        return (z * 4 + (x % 2) * 2 + c) * 8 + (x // 2) * 4 + y

                    out.append(
                        (
                            flat(z, x, y, c),
                            flat((z + dz) % 4, (x + dx) % 4, (y + dy) % 4, (c + dc) % 2),
                        )
                    )
    return out


def send(a, **k):
    return lax.ppermute(a, ("grp", "sp"), pairs(**k))


def call(body, outs, scratch, flops, nbytes, in_specs, out_specs):
    return pl.pallas_call(
        body,
        out_shape=outs,
        in_specs=in_specs,
        out_specs=out_specs,
        scratch_shapes=scratch,
        compiler_params=pltpu.CompilerParams(vmem_limit_bytes=VM),
        cost_estimate=pl.CostEstimate(flops=flops, bytes_accessed=nbytes, transcendentals=0),
    )


def run_copies(todo, sems):
    made = [pltpu.make_async_copy(a, b, sems.at[i]) for i, (a, b) in enumerate(todo)]
    for m in made:
        m.start()
    for m in made:
        m.wait()


def mult(i, n):
    return pl.multiple_of(i * n, n)


def pack_heads(h, queries, keys, values, grads, ids):
    extra = 128 if h == 0 else 0

    def body(q, k, v, g, i, o1, o2, o3, o0, sems):
        y = place()["y"]
        todo = []
        for d, o in ((1, o1), (2, o2), (3, o3), (0, o0)):
            s = h * 4 + lax.rem(y + d, 4)
            at = 0
            if d:
                todo += [
                    (q.at[0, :, pl.ds(mult(s, 512), 512)], o.at[:, 0:512]),
                    (g.at[0, :, pl.ds(mult(s, 512), 512)], o.at[:, 512:1024]),
                ]
                at = 1024
            todo += [
                (k.at[0, :, pl.ds(mult(s, 128), 128)], o.at[:, at : at + 128]),
                (v.at[0, :, pl.ds(mult(s, 128), 128)], o.at[:, at + 128 : at + 256]),
            ]
            if h == 0:
                todo.append((i, o.at[:, at + 256 : at + 384]))
        run_copies(todo, sems)

    shape = jax.ShapeDtypeStruct((128, 1280 + extra), BF16)
    return call(
        body,
        [shape] * 3 + [jax.ShapeDtypeStruct((128, 256 + extra), BF16)],
        [pltpu.SemaphoreType.DMA((19,))],
        0,
        4 * 10**6,
        [ANY] * 5,
        [VMEM] * 4,
    )(queries, keys, values, grads, ids)


def pack_inputs(hidden):
    def body(x, *refs):
        keep, give, sems = refs[:NJ], refs[NJ : 2 * NJ], refs[2 * NJ]
        c = place()["c"]
        todo = []
        for j in range(NJ):
            for b in range(8):
                for o, cc in ((keep[j], c), (give[j], 1 - c)):
                    col = pl.multiple_of((b * 2 + cc) * 256 + j * BW, BW)
                    todo.append((x.at[0, :, pl.ds(col, BW)], o.at[:, b * BW : (b + 1) * BW]))
        run_copies(todo, sems)

    shape = jax.ShapeDtypeStruct((128, 8 * BW), BF16)
    return call(
        body,
        [shape] * (2 * NJ),
        [pltpu.SemaphoreType.DMA((16 * NJ,))],
        0,
        4 * 10**6,
        [ANY],
        [VMEM] * (2 * NJ),
    )(hidden)


def attention(h, queries, grads, own, pieces, before, own0, pieces0, before0):
    def body(q, g, kv, p1, p2, p3, pv, kv0, i1, i2, i3, pv0, dq, dkv, dprev, qs, gs, ks, vs, ids, bias, acck, accv, sems):
        here = place()
        y, xh = here["y"], here["xh"]
        s = h * 4 + y
        row = mult(y, 128)
        todo = [
            (q.at[0, :, pl.ds(mult(s, 512), 512)], qs.at[pl.ds(row, 128), :]),
            (g.at[0, :, pl.ds(mult(s, 512), 512)], gs.at[pl.ds(row, 128), :]),
            (kv.at[:, 0:128], ks.at[pl.ds(row + 512, 128), :]),
            (kv.at[:, 128:256], vs.at[pl.ds(row + 512, 128), :]),
            (kv0.at[:, 256:384], ids.at[pl.ds(row + 512, 128), :]),
        ]
        for d, p, i in ((1, p1, i1), (2, p2, i2), (3, p3, i3)):
            r = mult(lax.rem(y - d + 4, 4), 128)
            todo += [
                (p.at[:, 0:512], qs.at[pl.ds(r, 128), :]),
                (p.at[:, 512:1024], gs.at[pl.ds(r, 128), :]),
                (p.at[:, 1024:1152], ks.at[pl.ds(r + 512, 128), :]),
                (p.at[:, 1152:1280], vs.at[pl.ds(r + 512, 128), :]),
                (i.at[:, 1280:1408], ids.at[pl.ds(r + 512, 128), :]),
            ]
        for d in range(4):
            r = mult(lax.rem(y - d + 4, 4), 128)
            here_rows = pl.ds(d * 128, 128)
            todo += [
                (pv.at[here_rows, 0:128], ks.at[pl.ds(r, 128), :]),
                (pv.at[here_rows, 128:256], vs.at[pl.ds(r, 128), :]),
                (pv0.at[here_rows, 256:384], ids.at[pl.ds(r, 128), :]),
            ]
        run_copies(todo, sems)

        low = xh * 512
        own_ids = ids[512:1024, :].astype(F32)
        prev_ids = ids[0:512, :].astype(F32)
        second = xh.astype(F32)

        def count(top):
            a = jnp.sum(jnp.where(own_ids <= top, 1.0, 0.0), axis=0, keepdims=True)
            b = jnp.sum(jnp.where(prev_ids <= top, 1.0, 0.0), axis=0, keepdims=True)
            return (a + second * b)[:, 0:1].astype(jnp.int32)

        first, both = count(0.5), count(1.5)
        acck[...] = jnp.zeros_like(acck)
        accv[...] = jnp.zeros_like(accv)
        for blk in range(2):
            lo = blk * 256
            t = lax.broadcasted_iota(jnp.int32, (1, 256), 1) + lo
            ta = t + low
            start = jnp.where(ta < first, 0, jnp.where(ta < both, first, both)) - low
            u = lax.broadcasted_iota(jnp.int32, (768, 256), 0) + (lo - 512)
            bias[blk] = jnp.where((u <= t) & (u >= start), 0.0, NEG)

        def head(hq, _):
            cols = pl.ds(mult(hq, 128), 128)
            for blk in range(2):
                lo = blk * 256
                keys = ks[lo : lo + 768, :]
                vals = vs[lo : lo + 768, :]
                qq = qs[lo : lo + 256, cols]
                gg = gs[lo : lo + 256, cols]
                nt = (((1,), (1,)), ((), ()))
                sc = lax.dot_general(keys, qq, nt, preferred_element_type=F32) * SCALE + bias[blk]
                e = jnp.exp(sc - jnp.max(sc, axis=0, keepdims=True))
                p = e * (1.0 / jnp.sum(e, axis=0, keepdims=True))
                p_low = p.astype(BF16)
                dp = lax.dot_general(vals, gg, nt, preferred_element_type=F32)
                delta = jnp.sum(p_low.astype(F32) * dp, axis=0, keepdims=True)
                ds = (p * (dp - delta) * SCALE).astype(BF16)
                tn = (((0,), (0,)), ((), ()))
                dqt = lax.dot_general(keys, ds, tn, preferred_element_type=F32)
                dq[cols, lo : lo + 256] = dqt.astype(BF16)
                acck[lo : lo + 768, :] += jnp.dot(ds, qq, preferred_element_type=F32)
                accv[lo : lo + 768, :] += jnp.dot(p_low, gg, preferred_element_type=F32)
            return 0

        lax.fori_loop(0, 4, head, 0)
        dkv[0:128, :] = acck[512:1024, :].T
        dkv[128:256, :] = accv[512:1024, :].T
        dprev[0:128, :] = acck[0:512, :].astype(BF16).T
        dprev[128:256, :] = accv[0:512, :].astype(BF16).T

    return call(
        body,
        [
            jax.ShapeDtypeStruct((512, 512), BF16),
            jax.ShapeDtypeStruct((256, 512), F32),
            jax.ShapeDtypeStruct((256, 512), BF16),
        ],
        [
            pltpu.VMEM((512, 512), BF16),
            pltpu.VMEM((512, 512), BF16),
            pltpu.VMEM((1024, 128), BF16),
            pltpu.VMEM((1024, 128), BF16),
            pltpu.VMEM((1024, 128), BF16),
            pltpu.VMEM((2, 768, 256), F32),
            pltpu.VMEM((1024, 128), F32),
            pltpu.VMEM((1024, 128), F32),
            pltpu.SemaphoreType.DMA((32,)),
        ],
        4 * 10**9,
        4 * 10**6,
        [ANY] * 12,
        [VMEM] * 3,
    )(queries, grads, own, *pieces, before, own0, *pieces0, before0)


def load_inputs(refs, xs, y):
    own, r1, r3, r2a, r2b = refs

    def at(d, half):
        return xs.at[pl.ds(pl.multiple_of(lax.rem(y - d + 4, 4) * 128 + half * 512, 128), 128), :]

    todo = []
    for d, r in ((0, own), (1, r1), (3, r3)):
        todo += [(r.at[0:128, :], at(d, 0)), (r.at[128:256, :], at(d, 1))]
    return todo + [(r2a, at(2, 0)), (r2b, at(2, 1))]


def weights_a(gt, inputs):
    def body(a0, b0, a1, b1, i0, i1, i2, i3, i4, o0, o1, o2, o3, xs, gs, sems):
        here = place()
        todo = load_inputs((i0, i1, i2, i3, i4), xs, here["y"])
        for h, (a, b) in enumerate(((a0, b0), (a1, b1))):
            todo += [
                (a.at[0:384, :], gs.at[h * 384 : (h + 1) * 384, 0:512]),
                (b.at[0:384, :], gs.at[h * 384 : (h + 1) * 384, 512:1024]),
            ]
        run_copies(todo, sems)
        for d, o in ((1, o1), (2, o2), (3, o3), (0, o0)):
            col = mult(lax.rem(here["z"] + d, 4), 2 * BW)
            o[...] = jnp.dot(
                gs[...], xs[:, pl.ds(col, 2 * BW)], preferred_element_type=F32
            ).astype(o.dtype)

    return call(
        body,
        [jax.ShapeDtypeStruct((768, 2 * BW), F32 if d == 0 else BF16) for d in range(4)],
        [
            pltpu.VMEM((1024, 8 * BW), BF16),
            pltpu.VMEM((768, 1024), BF16),
            pltpu.SemaphoreType.DMA((12,)),
        ],
        3 * 10**9 // NJ,
        8 * 10**6 // NJ,
        [ANY] * 9,
        [VMEM] * 4,
    )(*gt, *inputs)


def weights_b(gt, kvt, inputs):
    def body(a0, b0, a1, b1, k0, l0, k1, l1, i0, i1, i2, i3, i4, o0, o1, o2, o3, xs, gs, sems):
        here = place()
        todo = load_inputs((i0, i1, i2, i3, i4), xs, here["y"])
        for h, (a, b, k, l) in enumerate(((a0, b0, k0, l0), (a1, b1, k1, l1))):
            todo += [
                (a.at[384:512, :], gs.at[h, 0:128, 0:512]),
                (b.at[384:512, :], gs.at[h, 0:128, 512:1024]),
                (k, gs.at[h, 128:384, 0:512]),
                (l, gs.at[h, 128:384, 512:1024]),
            ]
        run_copies(todo, sems)
        for d, o in ((1, o1), (2, o2), (3, o3), (0, o0)):
            to = lax.rem(here["x"] + d, 4)
            lhs = gs[to // 2]
            for z in range(4):
                col = pl.multiple_of(z * 2 * BW + lax.rem(to, 2) * BW, BW)
                o[:, z * BW : (z + 1) * BW] = jnp.dot(
                    lhs, xs[:, pl.ds(col, BW)], preferred_element_type=F32
                ).astype(o.dtype)

    return call(
        body,
        [jax.ShapeDtypeStruct((384, 4 * BW), F32 if d == 0 else BF16) for d in range(4)],
        [
            pltpu.VMEM((1024, 8 * BW), BF16),
            pltpu.VMEM((2, 384, 1024), BF16),
            pltpu.SemaphoreType.DMA((16,)),
        ],
        3 * 10**9 // NJ,
        8 * 10**6 // NJ,
        [ANY] * 13,
        [VMEM] * 4,
    )(*gt, *kvt, *inputs)


def add_a(own, got):
    def body(o, r1, r2, r3, m0, m1, m2, m3, tot):
        x = place()["x"]
        tot[...] = o[...] + r1[...].astype(F32) + r2[...].astype(F32) + r3[...].astype(F32)
        for d, m in ((1, m1), (2, m2), (3, m3), (0, m0)):
            to = lax.rem(x + d, 4)
            m[...] = tot[
                pl.ds(mult(to // 2, 384), 384), pl.ds(mult(lax.rem(to, 2), BW), BW)
            ].astype(m.dtype)

    return call(
        body,
        [jax.ShapeDtypeStruct((384, BW), F32 if d == 0 else BF16) for d in range(4)],
        [pltpu.VMEM((768, 2 * BW), F32)],
        10**6,
        6 * 10**6 // NJ,
        [VMEM] * 4,
        [VMEM] * 4,
    )(own, *got)


def add_b(own, got):
    def body(o, r1, r2, r3, m0, m1, m2, m3, tot):
        z = place()["z"]
        tot[...] = o[...] + r1[...].astype(F32) + r2[...].astype(F32) + r3[...].astype(F32)
        for d, m in ((1, m1), (2, m2), (3, m3), (0, m0)):
            m[...] = tot[:, pl.ds(mult(lax.rem(z + d, 4), BW), BW)].astype(m.dtype)

    return call(
        body,
        [jax.ShapeDtypeStruct((384, BW), F32 if d == 0 else BF16) for d in range(4)],
        [pltpu.VMEM((384, 4 * BW), F32)],
        10**6,
        6 * 10**6 // NJ,
        [VMEM] * 4,
        [VMEM] * 4,
    )(own, *got)


def finish(parts):
    def body(*refs):
        ins, (qo, ko, vo) = refs[: 8 * NJ], refs[8 * NJ :]
        for j in range(NJ):
            a0, a1, a2, a3, b0, b1, b2, b3 = ins[j * 8 : (j + 1) * 8]
            rows = slice(j * BW, (j + 1) * BW)

            def total(r0, r1, r2, r3):
                t = r0[...] + r1[...].astype(F32) + r2[...].astype(F32) + r3[...].astype(F32)
                return (t * FACTOR).T

            a = total(a0, a1, a2, a3)
            b = total(b0, b1, b2, b3)
            qo[rows, 0:384] = a
            qo[rows, 384:512] = b[:, 0:128]
            ko[rows, :] = b[:, 128:256]
            vo[rows, :] = b[:, 256:384]

    return call(
        body,
        [
            jax.ShapeDtypeStruct((256, 512), F32),
            jax.ShapeDtypeStruct((256, 128), F32),
            jax.ShapeDtypeStruct((256, 128), F32),
        ],
        [],
        10**6,
        3 * 10**6,
        [VMEM] * (8 * NJ),
        [VMEM] * 3,
    )(*parts)


def per_device(hidden_in, queries, key_heads, saved_value_heads, out_grads, doc_ids):
    ids = jnp.broadcast_to(doc_ids.reshape(128, 1).astype(BF16), (128, 128))
    own, pieces, before = [], [], []
    for h in range(2):
        *msgs, kv = pack_heads(h, queries, key_heads, saved_value_heads, out_grads, ids)
        pieces.append([send(m, dy=d + 1) for d, m in enumerate(msgs)])
        own.append(kv)
    packed = pack_inputs(hidden_in)
    gathered = []
    for j in range(NJ):
        mine = jnp.concatenate([packed[j], send(packed[NJ + j], dc=1)], axis=0)
        r1 = send(mine, dy=1)
        r3 = send(mine, dy=-1)
        r2a = send(r1[0:128], dy=1)
        r2b = send(r3[128:256], dy=-1)
        gathered.append((mine, r1, r3, r2a, r2b))
    for h in range(2):
        kv = jnp.concatenate([own[h]] + [p[:, 1024:] for p in pieces[h]], axis=0)
        before.append(send(kv, dx=2, only_half=0))
    gt, kvt = [], []
    for h in range(2):
        dq, dkv, dprev = attention(
            h, queries, out_grads, own[h], pieces[h], before[h], own[0], pieces[0], before[0]
        )
        gt += [dq, send(dq, dc=1)]
        low = (dkv + send(dprev, dx=2, only_half=1).astype(F32)).astype(BF16)
        kvt += [low, send(low, dc=1)]
    parts = []
    for j in range(NJ):
        pa = weights_a(gt, gathered[j])
        got_a = [send(pa[d], dz=d) for d in (1, 2, 3)]
        pb = weights_b(gt, kvt, gathered[j])
        got_b = [send(pb[d], dx=d) for d in (1, 2, 3)]
        ma = add_a(pa[0], got_a)
        fa = [send(ma[d], dx=d) for d in (1, 2, 3)]
        mb = add_b(pb[0], got_b)
        fb = [send(mb[d], dz=d) for d in (1, 2, 3)]
        parts += [ma[0], *fa, mb[0], *fb]
    return finish(parts)


def solution(mesh):
    return jax.shard_map(
        per_device,
        mesh=mesh,
        in_specs=(
            P("grp", "sp", None),
            P("grp", "sp", None),
            P("grp", "sp", None),
            P("grp", "sp", None),
            P("grp", "sp", None),
            P("grp", "sp"),
        ),
        out_specs=(P("grp", "sp"), P("grp", "sp"), P("grp", "sp")),
        check_vma=False,
    )
```

```python
import math

import jax
import jax.numpy as jnp
from jax import lax
from jax.experimental import pallas as pl
from jax.experimental.pallas import tpu as pltpu
from jax.sharding import PartitionSpec as P

HEAD = 128
NEG = -1e30
SCALE = 1.0 / math.sqrt(HEAD)
FACTOR = 16384 ** -0.5
BW = 256
VM = 32 * 1024 * 1024
BIG = 60 * 1024 * 1024
F32 = jnp.float32
BF16 = jnp.bfloat16
ANY = pl.BlockSpec(memory_space=pl.ANY)
VMEM = pl.BlockSpec(memory_space=pltpu.VMEM)


def place():
    g = lax.axis_index("grp")
    s = lax.axis_index("sp")
    return dict(
        z=g // 4, x=(s // 4) * 2 + (g // 2) % 2, c=lax.rem(g, 2), y=lax.rem(s, 4), xh=s // 4
    )


def pairs(dx=0, dy=0, dz=0, dc=0, only_half=None):
    out = []
    for z in range(4):
        for x in range(4):
            for y in range(4):
                for c in range(2):
                    if only_half is not None and x // 2 != only_half:
                        continue

                    def flat(z, x, y, c):
                        return (z * 4 + (x % 2) * 2 + c) * 8 + (x // 2) * 4 + y

                    out.append(
                        (
                            flat(z, x, y, c),
                            flat((z + dz) % 4, (x + dx) % 4, (y + dy) % 4, (c + dc) % 2),
                        )
                    )
    return out


def send(label, a, **k):
    with jax.named_scope(label):
        return lax.ppermute(a, ("grp", "sp"), pairs(**k))


def call(body, outs, scratch, flops, nbytes, in_specs, out_specs, vm=VM):
    return pl.pallas_call(
        body,
        name=body.__name__,
        out_shape=outs,
        in_specs=in_specs,
        out_specs=out_specs,
        scratch_shapes=scratch,
        compiler_params=pltpu.CompilerParams(vmem_limit_bytes=vm),
        cost_estimate=pl.CostEstimate(flops=flops, bytes_accessed=nbytes, transcendentals=0),
    )


def run_copies(todo, sems):
    made = [pltpu.make_async_copy(a, b, sems.at[i]) for i, (a, b) in enumerate(todo)]
    for m in made:
        m.start()
    for m in made:
        m.wait()


def mult(i, n):
    return pl.multiple_of(i * n, n)


def pack_heads(queries, keys, values, grads, ids):
    def pack_heads_body(q, k, v, g, i, k1, k2, k3, k0, q1, q2, q3, sems):
        y = place()["y"]
        todo = []
        for d, ko, qo in ((1, k1, q1), (3, k3, q3), (2, k2, q2), (0, k0, None)):
            for h in range(2):
                s = h * 4 + lax.rem(y + d, 4)
                cols = pl.ds(mult(s, 128), 128)
                todo += [
                    (k.at[0, :, cols], ko.at[:, h * 256 : h * 256 + 128]),
                    (v.at[0, :, cols], ko.at[:, h * 256 + 128 : h * 256 + 256]),
                ]
                if d:
                    cols = pl.ds(mult(s, 512), 512)
                    todo += [
                        (q.at[0, :, cols], qo.at[:, h * 1024 : h * 1024 + 512]),
                        (g.at[0, :, cols], qo.at[:, h * 1024 + 512 : h * 1024 + 1024]),
                    ]
        spread = jnp.broadcast_to(i[...].astype(F32), (128, 128)).T.astype(BF16)
        for o in (k1, k2, k3, k0):
            o[:, 512:640] = spread
        run_copies(todo, sems)

    return call(
        pack_heads_body,
        [jax.ShapeDtypeStruct((128, 640), BF16)] * 4 + [jax.ShapeDtypeStruct((128, 2048), BF16)] * 3,
        [pltpu.SemaphoreType.DMA((28,))],
        10**8,
        10**6,
        [ANY] * 4 + [VMEM],
        [VMEM] * 7,
        BIG,
    )(queries, keys, values, grads, ids)


def pack_inputs(hidden):
    def pack_inputs_body(x, keep, give, sems):
        c = place()["c"]
        todo = []
        for b in range(8):
            at = (b % 2) * 4 + b // 2
            for o, cc in ((keep, c), (give, 1 - c)):
                cols = pl.ds(mult(b * 2 + cc, BW), BW)
                todo.append((x.at[0, :, cols], o.at[:, at * BW : (at + 1) * BW]))
        run_copies(todo, sems)

    shape = jax.ShapeDtypeStruct((128, 8 * BW), BF16)
    return call(
        pack_inputs_body,
        [shape] * 2,
        [pltpu.SemaphoreType.DMA((16,))],
        10**9,
        10**6,
        [ANY],
        [VMEM] * 2,
        BIG,
    )(hidden)


def attention(h, queries, grads, own, msgs, keys, before):
    def attention_body(q, g, kv, q1, q2, q3, k1, k2, k3, pv, pi, dq, dkv, dprev, qs, gs, ks, vs, ids, bias, acck, accv, sems):
        here = place()
        y, xh = here["y"], here["xh"]
        s = h * 4 + y
        row = mult(y, 128)
        todo = [
            (q.at[0, :, pl.ds(mult(s, 512), 512)], qs.at[pl.ds(row, 128), :]),
            (g.at[0, :, pl.ds(mult(s, 512), 512)], gs.at[pl.ds(row, 128), :]),
        ]
        for d, m, k in ((0, None, kv), (1, q1, k1), (2, q2, k2), (3, q3, k3)):
            r = mult(lax.rem(y - d + 4, 4), 128)
            if d:
                todo += [
                    (m.at[:, h * 1024 : h * 1024 + 512], qs.at[pl.ds(r, 128), :]),
                    (m.at[:, h * 1024 + 512 : h * 1024 + 1024], gs.at[pl.ds(r, 128), :]),
                ]
            todo += [
                (k.at[:, h * 256 : h * 256 + 128], ks.at[pl.ds(r + 512, 128), :]),
                (k.at[:, h * 256 + 128 : h * 256 + 256], vs.at[pl.ds(r + 512, 128), :]),
                (k.at[:, 512:640], ids.at[pl.ds(r + 512, 128), :]),
            ]
            rows = pl.ds(d * 128, 128)
            todo += [
                (pv.at[rows, 0:128], ks.at[pl.ds(r, 128), :]),
                (pv.at[rows, 128:256], vs.at[pl.ds(r, 128), :]),
                (pi.at[rows, 256:384], ids.at[pl.ds(r, 128), :]),
            ]
        run_copies(todo, sems)

        low = xh * 512
        own_ids = ids[512:1024, :].astype(F32)
        prev_ids = ids[0:512, :].astype(F32)
        second = xh.astype(F32)

        def count(top):
            a = jnp.sum(jnp.where(own_ids <= top, 1.0, 0.0), axis=0, keepdims=True)
            b = jnp.sum(jnp.where(prev_ids <= top, 1.0, 0.0), axis=0, keepdims=True)
            return (a + second * b)[:, 0:1].astype(jnp.int32)

        first, both = count(0.5), count(1.5)
        acck[...] = jnp.zeros_like(acck)
        accv[...] = jnp.zeros_like(accv)
        for blk in range(2):
            lo = blk * 256
            t = lax.broadcasted_iota(jnp.int32, (1, 256), 1) + lo
            ta = t + low
            start = jnp.where(ta < first, 0, jnp.where(ta < both, first, both)) - low
            u = lax.broadcasted_iota(jnp.int32, (768, 256), 0) + (lo - 512)
            bias[blk] = jnp.where((u <= t) & (u >= start), 0.0, NEG)

        def head(hq, _):
            cols = pl.ds(mult(hq, 128), 128)
            for blk in range(2):
                lo = blk * 256
                keys = ks[lo : lo + 768, :]
                vals = vs[lo : lo + 768, :]
                qq = qs[lo : lo + 256, cols]
                gg = gs[lo : lo + 256, cols]
                nt = (((1,), (1,)), ((), ()))
                sc = lax.dot_general(keys, qq, nt, preferred_element_type=F32) * SCALE + bias[blk]
                e = jnp.exp(sc - jnp.max(sc, axis=0, keepdims=True))
                p = e * (1.0 / jnp.sum(e, axis=0, keepdims=True))
                p_low = p.astype(BF16)
                dp = lax.dot_general(vals, gg, nt, preferred_element_type=F32)
                delta = jnp.sum(p_low.astype(F32) * dp, axis=0, keepdims=True)
                ds = (p * (dp - delta) * SCALE).astype(BF16)
                tn = (((0,), (0,)), ((), ()))
                dqt = lax.dot_general(keys, ds, tn, preferred_element_type=F32)
                dq[cols, lo : lo + 256] = dqt.astype(BF16)
                acck[lo : lo + 768, :] += jnp.dot(ds, qq, preferred_element_type=F32)
                accv[lo : lo + 768, :] += jnp.dot(p_low, gg, preferred_element_type=F32)
            return 0

        lax.fori_loop(0, 4, head, 0)
        dkv[0:128, :] = acck[512:1024, :].T
        dkv[128:256, :] = accv[512:1024, :].T
        dprev[0:128, :] = acck[0:512, :].astype(BF16).T
        dprev[128:256, :] = accv[0:512, :].astype(BF16).T

    return call(
        attention_body,
        [
            jax.ShapeDtypeStruct((512, 512), BF16),
            jax.ShapeDtypeStruct((256, 512), F32),
            jax.ShapeDtypeStruct((256, 512), BF16),
        ],
        [
            pltpu.VMEM((512, 512), BF16),
            pltpu.VMEM((512, 512), BF16),
            pltpu.VMEM((1024, 128), BF16),
            pltpu.VMEM((1024, 128), BF16),
            pltpu.VMEM((1024, 128), BF16),
            pltpu.VMEM((2, 768, 256), F32),
            pltpu.VMEM((1024, 128), F32),
            pltpu.VMEM((1024, 128), F32),
            pltpu.SemaphoreType.DMA((32,)),
        ],
        10**9,
        10**6,
        [ANY] * 11,
        [VMEM] * 3,
    )(queries, grads, own, *msgs, *keys, before[1 - h], before[0])


def gather_a(gt):
    def gather_a_body(a0, b0, a1, b1, ga, sems):
        todo = []
        for h, pair in enumerate(((a0, b0), (a1, b1))):
            for i, src in enumerate(pair):
                to = ga.at[h * 384 : (h + 1) * 384, i * 512 : (i + 1) * 512]
                todo.append((src.at[0:384, :], to))
        run_copies(todo, sems)

    return call(
        gather_a_body,
        jax.ShapeDtypeStruct((768, 1024), BF16),
        [pltpu.SemaphoreType.DMA((4,))],
        10**8,
        10**6,
        [ANY] * 4,
        VMEM,
    )(*gt)


def gather_b(gt, kv):
    def gather_b_body(a0, b0, a1, b1, k, l, gb, sems):
        todo = []
        for h, pair in enumerate(((a0, b0), (a1, b1))):
            for i, (src, low) in enumerate(zip(pair, (k, l))):
                cols = slice(i * 512, (i + 1) * 512)
                todo += [
                    (src.at[384:512, :], gb.at[h * 384 : h * 384 + 128, cols]),
                    (low.at[h * 256 : (h + 1) * 256, :], gb.at[h * 384 + 128 : (h + 1) * 384, cols]),
                ]
        run_copies(todo, sems)

    return call(
        gather_b_body,
        jax.ShapeDtypeStruct((768, 1024), BF16),
        [pltpu.SemaphoreType.DMA((8,))],
        10**8,
        10**6,
        [ANY] * 6,
        VMEM,
    )(*gt, *kv)


def product(a, b):
    return jnp.dot(a, b, preferred_element_type=F32)


def z_cols(xs, z):
    return jnp.concatenate(
        [xs[:, pl.ds(mult(z, BW), BW)], xs[:, pl.ds(mult(z + 4, BW), BW)]], axis=1
    )


def far_a(ga, inputs):
    def far_a_body(g, own, r1, r3, r2a, r2b, xs, up, down, sems):
        here = place()
        y = here["y"]

        def at(d, half):
            row = lax.rem(y - d + 4, 4) * 128 + half * 512
            return xs.at[pl.ds(pl.multiple_of(row, 128), 128), :]

        todo = []
        for d, r in ((0, own), (1, r1), (3, r3)):
            todo += [(r.at[0:128, :], at(d, 0)), (r.at[128:256, :], at(d, 1))]
        run_copies(todo + [(r2a, at(2, 0)), (r2b, at(2, 1))], sems)
        p = product(g[...], z_cols(xs, lax.rem(here["z"] + 2, 4)))
        up[...] = p[:, 0:BW].astype(BF16)
        down[...] = p[:, BW:].astype(BF16)

    return call(
        far_a_body,
        [jax.ShapeDtypeStruct((1024, 8 * BW), BF16)] + [jax.ShapeDtypeStruct((768, BW), BF16)] * 2,
        [pltpu.SemaphoreType.DMA((8,))],
        10**9,
        10**6,
        [VMEM] + [ANY] * 5,
        [VMEM] * 3,
    )(ga, *inputs)


def x_product(g, xs, to, lo, size):
    cols = xs[:, pl.ds(mult(lax.rem(to, 2) * 4 + lo, BW), size * BW)]
    return product(g[pl.ds(mult(to // 2, 384), 384), :], cols)


def far_b(gb, xs):
    def far_b_body(g, x, up, down):
        to = lax.rem(place()["x"] + 2, 4)
        for o, lo in ((up, 0), (down, 2)):
            o[...] = x_product(g, x, to, lo, 2).astype(BF16)

    return call(
        far_b_body,
        [jax.ShapeDtypeStruct((384, 2 * BW), BF16)] * 2,
        [],
        10**9,
        10**6,
        [VMEM] * 2,
        [VMEM] * 2,
    )(gb, xs)


def near_a(ga, xs):
    def near_a_body(g, x, up, down, own):
        z = place()["z"]
        for o, d in ((up, 1), (down, 3), (own, 0)):
            o[...] = product(g[...], z_cols(x, lax.rem(z + d, 4)))

    return call(
        near_a_body,
        [jax.ShapeDtypeStruct((768, 2 * BW), F32)] * 3,
        [],
        10**9,
        10**6,
        [VMEM] * 2,
        [VMEM] * 3,
    )(ga, xs)


def near_b(gb, xs):
    def near_b_body(g, x, up, down, own):
        for o, d in ((up, 1), (down, 3), (own, 0)):
            o[...] = x_product(g, x, lax.rem(place()["x"] + d, 4), 0, 4)

    return call(
        near_b_body,
        [jax.ShapeDtypeStruct((384, 4 * BW), F32)] * 3,
        [],
        10**9,
        10**6,
        [VMEM] * 2,
        [VMEM] * 3,
    )(gb, xs)


def add_near(up, down, got_up, got_down):
    rows, cols = up.shape
    half = cols // 2

    def add_near_body(u, d, gu, gd, ou, od):
        ou[:, 0:half] = (u[:, 0:half] + gu[...].astype(F32)).astype(BF16)
        ou[:, half:] = u[:, half:].astype(BF16)
        od[:, 0:half] = d[:, 0:half].astype(BF16)
        od[:, half:] = (d[:, half:] + gd[...].astype(F32)).astype(BF16)

    return call(
        add_near_body,
        [jax.ShapeDtypeStruct((rows, cols), BF16)] * 2,
        [],
        5 * 10**8,
        10**6,
        [VMEM] * 4,
        [VMEM] * 2,
    )(up, down, got_up, got_down)


def partial_shapes(*shape):
    return [jax.ShapeDtypeStruct(shape, F32 if d == 0 else BF16) for d in range(4)]


def total(refs):
    t = refs[0][...]
    for r in refs[1:]:
        t = t + r[...].astype(F32)
    return t


def add_a(parts):
    def add_a_body(*refs):
        outs, t = refs[3:7], refs[7]
        x = place()["x"]
        t[...] = total(refs[0:3])
        for d in range(4):
            to = lax.rem(x + d, 4)
            rows, cols = pl.ds(mult(to // 2, 384), 384), pl.ds(mult(lax.rem(to, 2), BW), BW)
            outs[d][...] = t[rows, cols].astype(outs[d].dtype)

    return call(
        add_a_body,
        partial_shapes(384, 256),
        [pltpu.VMEM((768, 2 * BW), F32)],
        5 * 10**8,
        10**6,
        [VMEM] * 3,
        [VMEM] * 4,
    )(*parts)


def add_b(parts):
    def add_b_body(*refs):
        outs, t = refs[3:7], refs[7]
        z = place()["z"]
        t[...] = total(refs[0:3])
        for d in range(4):
            o = outs[d]
            o[...] = t[:, pl.ds(mult(lax.rem(z + d, 4), BW), BW)].astype(o.dtype)

    return call(
        add_b_body,
        partial_shapes(384, 256),
        [pltpu.VMEM((384, 4 * BW), F32)],
        5 * 10**8,
        10**6,
        [VMEM] * 3,
        [VMEM] * 4,
    )(*parts)


def finish(parts):
    def finish_body(*refs):
        qo, ko, vo = refs[8:]
        a = (total(refs[0:4]) * FACTOR).T
        b = (total(refs[4:8]) * FACTOR).T
        qo[:, 0:384] = a
        qo[:, 384:512] = b[:, 0:128]
        ko[...] = b[:, 128:256]
        vo[...] = b[:, 256:384]

    return call(
        finish_body,
        [
            jax.ShapeDtypeStruct((256, 512), F32),
            jax.ShapeDtypeStruct((256, 128), F32),
            jax.ShapeDtypeStruct((256, 128), F32),
        ],
        [],
        0,
        0,
        [VMEM] * 8,
        [VMEM] * 3,
    )(*parts)


def after(x, *deps):
    return lax.optimization_barrier((x, *deps))[0]


def ring(label, far, up, down, **axis):
    step = {k: -v for k, v in axis.items()}
    got_up = send(label + "_far_up", far[0], **axis)
    got_down = send(label + "_far_down", far[1], **step)
    ou, od = add_near(up, down, got_up, got_down)
    return send(label + "_up", ou, **axis), send(label + "_down", od, **step)


def per_device(hidden_in, queries, key_heads, saved_value_heads, out_grads, doc_ids):
    *kmsg, own, q1, q2, q3 = pack_heads(queries, key_heads, saved_value_heads, out_grads, doc_ids)
    keys = [send("keys_y%d" % (d + 1), m, dy=d + 1) for d, m in enumerate(kmsg)]
    keep, give = pack_inputs(after(hidden_in, own))
    got = send("swap_inputs", give, dc=1)
    m1 = send("queries_y1", after(q1, keys[0]), dy=1)
    m3 = send("queries_y3", after(q3, keys[0], keys[2]), dy=3)
    m2 = send("queries_y2", after(q2, keys[0], keys[2], got), dy=2)
    msgs = [m1, m2, m3]
    all_keys = jnp.concatenate([own] + keys, axis=0)
    before = [
        send("half0", all_keys[:, 256:640], dx=2, only_half=0),
        send("half1", all_keys[:, 0:256], dx=2, only_half=0),
    ]
    mine = jnp.concatenate([keep, got], axis=0)
    sent = after(mine, m1, m3)
    up = send("inputs_up", sent, dy=1)
    down = send("inputs_down", sent, dy=-1)

    dq0, dkv0, back0 = attention(0, queries, out_grads, own, msgs, keys, before)
    swap0 = send("swap_dq0", dq0, dc=1)
    dq1, dkv1, back1 = attention(1, after(queries, dq0, swap0), out_grads, own, msgs, keys, before)
    fwd = send("inputs_up2", after(up[0:128], dq1), dy=1)
    rev = send("inputs_down2", after(down[128:256], dq1), dy=-1)
    swap1 = send("swap_dq1", dq1, dc=1)
    ret = send("back", jnp.concatenate([back0, back1], axis=0), dx=2, only_half=1)
    ret = after(ret, fwd, rev, swap1).astype(F32)
    low = (jnp.concatenate([dkv0, dkv1], axis=0) + ret).astype(BF16)
    kv = (low, send("swap_dkv", low, dc=1))
    inputs = (mine, up, down, fwd, rev)
    gt = (dq0, swap0, dq1, swap1)

    ga = gather_a(gt)
    xs, *fa = far_a(ga, inputs)
    gb = gather_b(gt, kv)
    fb = far_b(after(gb, fa[0]), xs)
    ua, da, oa = near_a(after(ga, fb[0]), xs)
    ub, db, ob = near_b(after(gb, oa), xs)
    ra = ring("reduce_a", fa, ua, da, dz=1)
    rb = ring("reduce_b", fb, ub, db, dx=1)
    ma = add_a([oa, *ra])
    sa = [send("second_a_x%d" % d, ma[d], dx=d) for d in (1, 3, 2)]
    mb = add_b([ob, *rb])
    sb = [send("second_b_z%d" % d, mb[d], dz=d) for d in (1, 3, 2)]
    return finish([ma[0], *sa, mb[0], *sb])


def solution(mesh):
    return jax.shard_map(
        per_device,
        mesh=mesh,
        in_specs=(
            P("grp", "sp", None),
            P("grp", "sp", None),
            P("grp", "sp", None),
            P("grp", "sp", None),
            P("grp", "sp", None),
            P("grp", "sp"),
        ),
        out_specs=(P("grp", "sp"), P("grp", "sp"), P("grp", "sp")),
        check_vma=False,
    )
```

```python
import math

import jax
import jax.numpy as jnp
from jax import lax
from jax.experimental import pallas as pl
from jax.experimental.pallas import tpu as pltpu
from jax.sharding import PartitionSpec as P

HEAD = 128
NEG = -1e30
SCALE = 1.0 / math.sqrt(HEAD)
FACTOR = 16384 ** -0.5
BW = 256
VM = 32 * 1024 * 1024
BIG = 60 * 1024 * 1024
F32 = jnp.float32
BF16 = jnp.bfloat16
ANY = pl.BlockSpec(memory_space=pl.ANY)
VMEM = pl.BlockSpec(memory_space=pltpu.VMEM)


def place():
    g = lax.axis_index("grp")
    s = lax.axis_index("sp")
    return dict(
        z=g // 4, x=(s // 4) * 2 + (g // 2) % 2, c=lax.rem(g, 2), y=lax.rem(s, 4), xh=s // 4
    )


def pairs(dx=0, dy=0, dz=0, dc=0, only_half=None):
    out = []
    for z in range(4):
        for x in range(4):
            for y in range(4):
                for c in range(2):
                    if only_half is not None and x // 2 != only_half:
                        continue

                    def flat(z, x, y, c):
                        return (z * 4 + (x % 2) * 2 + c) * 8 + (x // 2) * 4 + y

                    out.append(
                        (
                            flat(z, x, y, c),
                            flat((z + dz) % 4, (x + dx) % 4, (y + dy) % 4, (c + dc) % 2),
                        )
                    )
    return out


def send(label, a, **k):
    with jax.named_scope(label):
        return lax.ppermute(a, ("grp", "sp"), pairs(**k))


def call(body, outs, scratch, flops, nbytes, in_specs, out_specs, vm=VM):
    return pl.pallas_call(
        body,
        name=body.__name__,
        out_shape=outs,
        in_specs=in_specs,
        out_specs=out_specs,
        scratch_shapes=scratch,
        compiler_params=pltpu.CompilerParams(vmem_limit_bytes=vm),
        cost_estimate=pl.CostEstimate(flops=flops, bytes_accessed=nbytes, transcendentals=0),
    )


def run_copies(todo, sems):
    made = [pltpu.make_async_copy(a, b, sems.at[i]) for i, (a, b) in enumerate(todo)]
    for m in made:
        m.start()
    for m in made:
        m.wait()


def mult(i, n):
    return pl.multiple_of(i * n, n)


def pack_heads(queries, keys, values, grads, ids):
    def pack_heads_body(q, k, v, g, i, k1, k2, k3, k0, *refs):
        qs, sems = refs[:6], refs[6]
        y = place()["y"]
        todo = []
        for d, o in ((1, k1), (3, k3), (2, k2), (0, k0)):
            for h in range(2):
                cols = pl.ds(mult(h * 4 + lax.rem(y + d, 4), 128), 128)
                todo += [
                    (k.at[0, :, cols], o.at[:, h * 256 : h * 256 + 128]),
                    (v.at[0, :, cols], o.at[:, h * 256 + 128 : h * 256 + 256]),
                ]
        for h in range(2):
            for d in (1, 2, 3):
                o = qs[h * 3 + d - 1]
                cols = pl.ds(mult(h * 4 + lax.rem(y + d, 4), 512), 512)
                todo += [(q.at[0, :, cols], o.at[:, 0:512]), (g.at[0, :, cols], o.at[:, 512:1024])]
        spread = jnp.broadcast_to(i[...].astype(F32), (128, 128)).T.astype(BF16)
        for o in (k1, k2, k3, k0):
            o[:, 512:640] = spread
        run_copies(todo, sems)

    return call(
        pack_heads_body,
        [jax.ShapeDtypeStruct((128, 640), BF16)] * 4 + [jax.ShapeDtypeStruct((128, 1024), BF16)] * 6,
        [pltpu.SemaphoreType.DMA((28,))],
        10**8,
        10**6,
        [ANY] * 4 + [VMEM],
        [VMEM] * 10,
        BIG,
    )(queries, keys, values, grads, ids)


def pack_inputs(hidden):
    def pack_inputs_body(x, keep, give, sems):
        c = place()["c"]
        todo = []
        for b in range(8):
            at = (b % 2) * 4 + b // 2
            for o, cc in ((keep, c), (give, 1 - c)):
                cols = pl.ds(mult(b * 2 + cc, BW), BW)
                todo.append((x.at[0, :, cols], o.at[:, at * BW : (at + 1) * BW]))
        run_copies(todo, sems)

    shape = jax.ShapeDtypeStruct((128, 8 * BW), BF16)
    return call(
        pack_inputs_body,
        [shape] * 2,
        [pltpu.SemaphoreType.DMA((16,))],
        10**9,
        10**6,
        [ANY],
        [VMEM] * 2,
        BIG,
    )(hidden)


def arrange(h, queries, grads, msgs):
    def arrange_body(q, g, q1, q2, q3, qs, gs, sems):
        y = place()["y"]
        cols, row = pl.ds(mult(h * 4 + y, 512), 512), pl.ds(mult(y, 128), 128)
        todo = [(q.at[0, :, cols], qs.at[row, :]), (g.at[0, :, cols], gs.at[row, :])]
        for d, m in ((1, q1), (2, q2), (3, q3)):
            row = pl.ds(mult(lax.rem(y - d + 4, 4), 128), 128)
            todo += [(m.at[:, 0:512], qs.at[row, :]), (m.at[:, 512:1024], gs.at[row, :])]
        run_copies(todo, sems)

    return call(
        arrange_body,
        [jax.ShapeDtypeStruct((512, 512), BF16)] * 2,
        [pltpu.SemaphoreType.DMA((8,))],
        6 * 10**9,
        10**6,
        [ANY] * 5,
        [VMEM] * 2,
    )(queries, grads, *msgs)


def attention(h, queries, grads, own, keys, before):
    def attention_body(qs, gs, kv, k1, k2, k3, pv, dq, dkv, dprev, ks, vs, ids, bias, acck, accv, sems):
        here = place()
        y, xh = here["y"], here["xh"]
        todo = []
        for d, k in ((0, kv), (1, k1), (2, k2), (3, k3)):
            r = mult(lax.rem(y - d + 4, 4), 128)
            todo += [
                (k.at[:, h * 256 : h * 256 + 128], ks.at[pl.ds(r + 512, 128), :]),
                (k.at[:, h * 256 + 128 : h * 256 + 256], vs.at[pl.ds(r + 512, 128), :]),
                (k.at[:, 512:640], ids.at[pl.ds(r + 512, 128), :]),
            ]
            rows = pl.ds(d * 128, 128)
            todo += [
                (pv.at[rows, h * 256 : h * 256 + 128], ks.at[pl.ds(r, 128), :]),
                (pv.at[rows, h * 256 + 128 : h * 256 + 256], vs.at[pl.ds(r, 128), :]),
                (pv.at[rows, 512:640], ids.at[pl.ds(r, 128), :]),
            ]
        run_copies(todo, sems)

        low = xh * 512
        own_ids = ids[512:1024, :].astype(F32)
        prev_ids = ids[0:512, :].astype(F32)
        second = xh.astype(F32)

        def count(top):
            a = jnp.sum(jnp.where(own_ids <= top, 1.0, 0.0), axis=0, keepdims=True)
            b = jnp.sum(jnp.where(prev_ids <= top, 1.0, 0.0), axis=0, keepdims=True)
            return (a + second * b)[:, 0:1].astype(jnp.int32)

        first, both = count(0.5), count(1.5)
        acck[...] = jnp.zeros_like(acck)
        accv[...] = jnp.zeros_like(accv)
        for blk in range(2):
            lo = blk * 256
            t = lax.broadcasted_iota(jnp.int32, (1, 256), 1) + lo
            ta = t + low
            start = jnp.where(ta < first, 0, jnp.where(ta < both, first, both)) - low
            u = lax.broadcasted_iota(jnp.int32, (768, 256), 0) + (lo - 512)
            bias[blk] = jnp.where((u <= t) & (u >= start), 0.0, NEG)

        def head(hq, _):
            cols = pl.ds(mult(hq, 128), 128)
            for blk in range(2):
                lo = blk * 256
                keys = ks[lo : lo + 768, :]
                vals = vs[lo : lo + 768, :]
                qq = qs[lo : lo + 256, cols]
                gg = gs[lo : lo + 256, cols]
                nt = (((1,), (1,)), ((), ()))
                sc = lax.dot_general(keys, qq, nt, preferred_element_type=F32) * SCALE + bias[blk]
                e = jnp.exp(sc - jnp.max(sc, axis=0, keepdims=True))
                p = e * (1.0 / jnp.sum(e, axis=0, keepdims=True))
                p_low = p.astype(BF16)
                dp = lax.dot_general(vals, gg, nt, preferred_element_type=F32)
                delta = jnp.sum(p_low.astype(F32) * dp, axis=0, keepdims=True)
                ds = (p * (dp - delta) * SCALE).astype(BF16)
                tn = (((0,), (0,)), ((), ()))
                dqt = lax.dot_general(keys, ds, tn, preferred_element_type=F32)
                dq[cols, lo : lo + 256] = dqt.astype(BF16)
                acck[lo : lo + 768, :] += jnp.dot(ds, qq, preferred_element_type=F32)
                accv[lo : lo + 768, :] += jnp.dot(p_low, gg, preferred_element_type=F32)
            return 0

        lax.fori_loop(0, 4, head, 0, unroll=4)
        dkv[0:128, :] = acck[512:1024, :].T
        dkv[128:256, :] = accv[512:1024, :].T
        dprev[0:128, :] = acck[0:512, :].astype(BF16).T
        dprev[128:256, :] = accv[0:512, :].astype(BF16).T

    return call(
        attention_body,
        [
            jax.ShapeDtypeStruct((512, 512), BF16),
            jax.ShapeDtypeStruct((256, 512), F32),
            jax.ShapeDtypeStruct((256, 512), BF16),
        ],
        [
            pltpu.VMEM((1024, 128), BF16),
            pltpu.VMEM((1024, 128), BF16),
            pltpu.VMEM((1024, 128), BF16),
            pltpu.VMEM((2, 768, 256), F32),
            pltpu.VMEM((1024, 128), F32),
            pltpu.VMEM((1024, 128), F32),
            pltpu.SemaphoreType.DMA((32,)),
        ],
        12 * 10**9,
        10**6,
        [VMEM] * 2 + [ANY] * 5,
        [VMEM] * 3,
    )(queries, grads, own, *keys, before)


def gather_a(gt):
    def gather_a_body(a0, b0, a1, b1, ga, sems):
        todo = []
        for h, pair in enumerate(((a0, b0), (a1, b1))):
            for i, src in enumerate(pair):
                to = ga.at[h * 384 : (h + 1) * 384, i * 512 : (i + 1) * 512]
                todo.append((src.at[0:384, :], to))
        run_copies(todo, sems)

    return call(
        gather_a_body,
        jax.ShapeDtypeStruct((768, 1024), BF16),
        [pltpu.SemaphoreType.DMA((4,))],
        10**8,
        10**6,
        [ANY] * 4,
        VMEM,
    )(*gt)


def gather_b(gt, kv):
    def gather_b_body(a0, b0, a1, b1, k, l, gb, sems):
        todo = []
        for h, pair in enumerate(((a0, b0), (a1, b1))):
            for i, (src, low) in enumerate(zip(pair, (k, l))):
                cols = slice(i * 512, (i + 1) * 512)
                todo += [
                    (src.at[384:512, :], gb.at[h * 384 : h * 384 + 128, cols]),
                    (low.at[h * 256 : (h + 1) * 256, :], gb.at[h * 384 + 128 : (h + 1) * 384, cols]),
                ]
        run_copies(todo, sems)

    return call(
        gather_b_body,
        jax.ShapeDtypeStruct((768, 1024), BF16),
        [pltpu.SemaphoreType.DMA((8,))],
        10**8,
        10**6,
        [ANY] * 6,
        VMEM,
    )(*gt, *kv)


def product(a, b):
    return jnp.dot(a, b, preferred_element_type=F32)


def z_cols(xs, z):
    return jnp.concatenate(
        [xs[:, pl.ds(mult(z, BW), BW)], xs[:, pl.ds(mult(z + 4, BW), BW)]], axis=1
    )


def far_a(ga, inputs):
    def far_a_body(g, own, r1, r3, r2a, r2b, xs, up, down, sems):
        here = place()
        y = here["y"]

        def at(d, half):
            row = lax.rem(y - d + 4, 4) * 128 + half * 512
            return xs.at[pl.ds(pl.multiple_of(row, 128), 128), :]

        todo = []
        for d, r in ((0, own), (1, r1), (3, r3)):
            todo += [(r.at[0:128, :], at(d, 0)), (r.at[128:256, :], at(d, 1))]
        run_copies(todo + [(r2a, at(2, 0)), (r2b, at(2, 1))], sems)
        p = product(g[...], z_cols(xs, lax.rem(here["z"] + 2, 4)))
        up[...] = p[:, 0:BW].astype(BF16)
        down[...] = p[:, BW:].astype(BF16)

    return call(
        far_a_body,
        [jax.ShapeDtypeStruct((1024, 8 * BW), BF16)] + [jax.ShapeDtypeStruct((768, BW), BF16)] * 2,
        [pltpu.SemaphoreType.DMA((8,))],
        10**9,
        10**6,
        [VMEM] + [ANY] * 5,
        [VMEM] * 3,
    )(ga, *inputs)


def x_product(g, xs, to, lo, size):
    cols = xs[:, pl.ds(mult(lax.rem(to, 2) * 4 + lo, BW), size * BW)]
    return product(g[pl.ds(mult(to // 2, 384), 384), :], cols)


def far_b(gb, xs):
    def far_b_body(g, x, up, down):
        to = lax.rem(place()["x"] + 2, 4)
        for o, lo in ((up, 0), (down, 2)):
            o[...] = x_product(g, x, to, lo, 2).astype(BF16)

    return call(
        far_b_body,
        [jax.ShapeDtypeStruct((384, 2 * BW), BF16)] * 2,
        [],
        10**9,
        10**6,
        [VMEM] * 2,
        [VMEM] * 2,
    )(gb, xs)


def near_a(ga, xs):
    def near_a_body(g, x, up, down, own):
        z = place()["z"]
        for o, d in ((up, 1), (down, 3), (own, 0)):
            o[...] = product(g[...], z_cols(x, lax.rem(z + d, 4)))

    return call(
        near_a_body,
        [jax.ShapeDtypeStruct((768, 2 * BW), F32)] * 3,
        [],
        10**9,
        10**6,
        [VMEM] * 2,
        [VMEM] * 3,
    )(ga, xs)


def near_b(gb, xs):
    def near_b_body(g, x, up, down, own):
        for o, d in ((up, 1), (down, 3), (own, 0)):
            o[...] = x_product(g, x, lax.rem(place()["x"] + d, 4), 0, 4)

    return call(
        near_b_body,
        [jax.ShapeDtypeStruct((384, 4 * BW), F32)] * 3,
        [],
        10**9,
        10**6,
        [VMEM] * 2,
        [VMEM] * 3,
    )(gb, xs)


def add_near(up, down, got_up, got_down):
    rows, cols = up.shape
    half = cols // 2

    def add_near_body(u, d, gu, gd, ou, od):
        ou[:, 0:half] = (u[:, 0:half] + gu[...].astype(F32)).astype(BF16)
        ou[:, half:] = u[:, half:].astype(BF16)
        od[:, 0:half] = d[:, 0:half].astype(BF16)
        od[:, half:] = (d[:, half:] + gd[...].astype(F32)).astype(BF16)

    return call(
        add_near_body,
        [jax.ShapeDtypeStruct((rows, cols), BF16)] * 2,
        [],
        5 * 10**8,
        10**6,
        [VMEM] * 4,
        [VMEM] * 2,
    )(up, down, got_up, got_down)


def partial_shapes(*shape):
    return [jax.ShapeDtypeStruct(shape, F32 if d == 0 else BF16) for d in range(4)]


def total(refs):
    t = refs[0][...]
    for r in refs[1:]:
        t = t + r[...].astype(F32)
    return t


def add_a(parts):
    def add_a_body(*refs):
        outs, t = refs[3:7], refs[7]
        x = place()["x"]
        t[...] = total(refs[0:3])
        for d in range(4):
            to = lax.rem(x + d, 4)
            rows, cols = pl.ds(mult(to // 2, 384), 384), pl.ds(mult(lax.rem(to, 2), BW), BW)
            outs[d][...] = t[rows, cols].astype(outs[d].dtype)

    return call(
        add_a_body,
        partial_shapes(384, 256),
        [pltpu.VMEM((768, 2 * BW), F32)],
        5 * 10**8,
        10**6,
        [VMEM] * 3,
        [VMEM] * 4,
    )(*parts)


def add_b(parts):
    def add_b_body(*refs):
        outs, t = refs[3:7], refs[7]
        z = place()["z"]
        t[...] = total(refs[0:3])
        for d in range(4):
            o = outs[d]
            o[...] = t[:, pl.ds(mult(lax.rem(z + d, 4), BW), BW)].astype(o.dtype)

    return call(
        add_b_body,
        partial_shapes(384, 256),
        [pltpu.VMEM((384, 4 * BW), F32)],
        5 * 10**8,
        10**6,
        [VMEM] * 3,
        [VMEM] * 4,
    )(*parts)


def finish(parts):
    def finish_body(*refs):
        qo, ko, vo = refs[8:]
        a = (total(refs[0:4]) * FACTOR).T
        b = (total(refs[4:8]) * FACTOR).T
        qo[:, 0:384] = a
        qo[:, 384:512] = b[:, 0:128]
        ko[...] = b[:, 128:256]
        vo[...] = b[:, 256:384]

    return call(
        finish_body,
        [
            jax.ShapeDtypeStruct((256, 512), F32),
            jax.ShapeDtypeStruct((256, 128), F32),
            jax.ShapeDtypeStruct((256, 128), F32),
        ],
        [],
        0,
        0,
        [VMEM] * 8,
        [VMEM] * 3,
    )(*parts)


def after(x, *deps):
    return lax.optimization_barrier((x, *deps))[0]


def ring(label, far, up, down, **axis):
    step = {k: -v for k, v in axis.items()}
    got_up = send(label + "_far_up", far[0], **axis)
    got_down = send(label + "_far_down", far[1], **step)
    ou, od = add_near(up, down, got_up, got_down)
    return send(label + "_up", ou, **axis), send(label + "_down", od, **step)


def per_device(hidden_in, queries, key_heads, saved_value_heads, out_grads, doc_ids):
    *kmsg, own, q01, q02, q03, q11, q12, q13 = pack_heads(
        queries, key_heads, saved_value_heads, out_grads, doc_ids
    )
    keys = [send("keys_y%d" % (d + 1), m, dy=d + 1) for d, m in enumerate(kmsg)]
    keep, give = pack_inputs(after(hidden_in, own))
    got = send("swap_inputs", give, dc=1)
    a1 = send("queries0_y1", after(q01, keys[0]), dy=1)
    a3 = send("queries0_y3", after(q03, keys[0], keys[2]), dy=3)
    a2 = send("queries0_y2", after(q02, keys[0], keys[2]), dy=2)
    before = send("half", jnp.concatenate([own] + keys, axis=0), dx=2)
    b1 = send("queries1_y1", after(q11, a1), dy=1)
    b3 = send("queries1_y3", after(q13, a1), dy=3)
    b2 = send("queries1_y2", after(q12, a1, a3), dy=2)
    sent = after(jnp.concatenate([keep, got], axis=0), a1, a2, a3)
    up = send("inputs_up", sent, dy=1)
    down = send("inputs_down", sent, dy=-1)

    def attend(h, dep, msgs):
        qs, gs = arrange(h, after(queries, *dep), out_grads, msgs)
        return attention(h, qs, gs, own, keys, before)

    dq0, dkv0, back0 = attend(0, (), (a1, a2, a3))
    swap0 = send("swap_dq0", dq0, dc=1)
    dq1, dkv1, back1 = attend(1, (dq0,), (b1, b2, b3))
    fwd = send("inputs_up2", after(up[0:128], dq1), dy=1)
    rev = send("inputs_down2", after(down[128:256], dq1), dy=-1)
    swap1 = send("swap_dq1", dq1, dc=1)
    ret = send("back", jnp.concatenate([back0, back1], axis=0), dx=2)
    ret = after(ret, fwd, rev, swap1).astype(F32)
    low = (jnp.concatenate([dkv0, dkv1], axis=0) + ret).astype(BF16)
    kv = (low, send("swap_dkv", low, dc=1))
    inputs = (sent, up, down, fwd, rev)
    gt = (dq0, swap0, dq1, swap1)

    ga = gather_a(gt)
    xs, *fa = far_a(ga, inputs)
    gb = gather_b(gt, kv)
    fb = far_b(after(gb, fa[0]), xs)
    ua, da, oa = near_a(after(ga, fb[0]), xs)
    ub, db, ob = near_b(after(gb, oa), xs)
    ra = ring("reduce_a", fa, ua, da, dz=1)
    rb = ring("reduce_b", fb, ub, db, dx=1)
    ma = add_a([oa, *ra])
    sa = [send("second_a_x%d" % d, ma[d], dx=d) for d in (1, 3, 2)]
    mb = add_b([ob, *rb])
    sb = [send("second_b_z%d" % d, mb[d], dz=d) for d in (1, 3, 2)]
    return finish([ma[0], *sa, mb[0], *sb])


def solution(mesh):
    return jax.shard_map(
        per_device,
        mesh=mesh,
        in_specs=(
            P("grp", "sp", None),
            P("grp", "sp", None),
            P("grp", "sp", None),
            P("grp", "sp", None),
            P("grp", "sp", None),
            P("grp", "sp"),
        ),
        out_specs=(P("grp", "sp"), P("grp", "sp"), P("grp", "sp")),
        check_vma=False,
    )
```

```python
import math

import jax
import jax.numpy as jnp
from jax import lax
from jax.experimental import pallas as pl
from jax.experimental.pallas import tpu as pltpu
from jax.sharding import PartitionSpec as P

HEAD = 128
NEG = -1e30
SCALE = 1.0 / math.sqrt(HEAD)
FACTOR = 16384 ** -0.5
BW = 256
VM = 32 * 1024 * 1024
BIG = 60 * 1024 * 1024
F32 = jnp.float32
BF16 = jnp.bfloat16
ANY = pl.BlockSpec(memory_space=pl.ANY)
VMEM = pl.BlockSpec(memory_space=pltpu.VMEM)


def place():
    g = lax.axis_index("grp")
    s = lax.axis_index("sp")
    return dict(
        z=g // 4, x=(s // 4) * 2 + (g // 2) % 2, c=lax.rem(g, 2), y=lax.rem(s, 4), xh=s // 4
    )


def pairs(dx=0, dy=0, dz=0, dc=0, only_half=None):
    out = []
    for z in range(4):
        for x in range(4):
            for y in range(4):
                for c in range(2):
                    if only_half is not None and x // 2 != only_half:
                        continue

                    def flat(z, x, y, c):
                        return (z * 4 + (x % 2) * 2 + c) * 8 + (x // 2) * 4 + y

                    out.append(
                        (
                            flat(z, x, y, c),
                            flat((z + dz) % 4, (x + dx) % 4, (y + dy) % 4, (c + dc) % 2),
                        )
                    )
    return out


def send(label, a, **k):
    with jax.named_scope(label):
        return lax.ppermute(a, ("grp", "sp"), pairs(**k))


def call(body, outs, scratch, flops, nbytes, in_specs, out_specs, vm=VM):
    return pl.pallas_call(
        body,
        name=body.__name__,
        out_shape=outs,
        in_specs=in_specs,
        out_specs=out_specs,
        scratch_shapes=scratch,
        compiler_params=pltpu.CompilerParams(vmem_limit_bytes=vm),
        cost_estimate=pl.CostEstimate(flops=flops, bytes_accessed=nbytes, transcendentals=0),
    )


def run_copies(todo, sems):
    made = [pltpu.make_async_copy(a, b, sems.at[i]) for i, (a, b) in enumerate(todo)]
    for m in made:
        m.start()
    for m in made:
        m.wait()


def mult(i, n):
    return pl.multiple_of(i * n, n)


def pack_heads(queries, keys, values, grads, ids):
    def pack_heads_body(q, k, v, g, i, k1, k2, k3, k0, *refs):
        qs, sems = refs[:6], refs[6]
        y = place()["y"]
        todo = []
        for d, o in ((1, k1), (3, k3), (2, k2), (0, k0)):
            for h in range(2):
                cols = pl.ds(mult(h * 4 + lax.rem(y + d, 4), 128), 128)
                todo += [
                    (k.at[0, :, cols], o.at[:, h * 256 : h * 256 + 128]),
                    (v.at[0, :, cols], o.at[:, h * 256 + 128 : h * 256 + 256]),
                ]
        for h in range(2):
            for d in (1, 2, 3):
                o = qs[h * 3 + d - 1]
                cols = pl.ds(mult(h * 4 + lax.rem(y + d, 4), 512), 512)
                todo += [(q.at[0, :, cols], o.at[:, 0:512]), (g.at[0, :, cols], o.at[:, 512:1024])]
        spread = jnp.broadcast_to(i[...].astype(F32), (128, 128)).T.astype(BF16)
        for o in (k1, k2, k3, k0):
            o[:, 512:640] = spread
        run_copies(todo, sems)

    return call(
        pack_heads_body,
        [jax.ShapeDtypeStruct((128, 640), BF16)] * 4 + [jax.ShapeDtypeStruct((128, 1024), BF16)] * 6,
        [pltpu.SemaphoreType.DMA((28,))],
        10**8,
        10**6,
        [ANY] * 4 + [VMEM],
        [VMEM] * 10,
        BIG,
    )(queries, keys, values, grads, ids)


def pack_inputs(hidden):
    def pack_inputs_body(x, keep, give, sems):
        c = place()["c"]
        todo = []
        for b in range(8):
            at = (b % 2) * 4 + b // 2
            for o, cc in ((keep, c), (give, 1 - c)):
                cols = pl.ds(mult(b * 2 + cc, BW), BW)
                todo.append((x.at[0, :, cols], o.at[:, at * BW : (at + 1) * BW]))
        run_copies(todo, sems)

    shape = jax.ShapeDtypeStruct((128, 8 * BW), BF16)
    return call(
        pack_inputs_body,
        [shape] * 2,
        [pltpu.SemaphoreType.DMA((16,))],
        10**9,
        10**6,
        [ANY],
        [VMEM] * 2,
        BIG,
    )(hidden)


def arrange(h, queries, grads, msgs):
    def arrange_body(q, g, q1, q2, q3, qs, gs, sems):
        y = place()["y"]
        cols, row = pl.ds(mult(h * 4 + y, 512), 512), pl.ds(mult(y, 128), 128)
        todo = [(q.at[0, :, cols], qs.at[row, :]), (g.at[0, :, cols], gs.at[row, :])]
        for d, m in ((1, q1), (2, q2), (3, q3)):
            row = pl.ds(mult(lax.rem(y - d + 4, 4), 128), 128)
            todo += [(m.at[:, 0:512], qs.at[row, :]), (m.at[:, 512:1024], gs.at[row, :])]
        run_copies(todo, sems)

    return call(
        arrange_body,
        [jax.ShapeDtypeStruct((512, 512), BF16)] * 2,
        [pltpu.SemaphoreType.DMA((8,))],
        6 * 10**9,
        10**6,
        [ANY] * 5,
        [VMEM] * 2,
    )(queries, grads, *msgs)


def attention(h, queries, grads, own, keys, before):
    def attention_body(qs, gs, kv, k1, k2, k3, pv, dq, dkv, dprev, ks, vs, ids, bias, acck, accv, sems):
        here = place()
        y, xh = here["y"], here["xh"]
        todo = []
        for d, k in ((0, kv), (1, k1), (2, k2), (3, k3)):
            r = mult(lax.rem(y - d + 4, 4), 128)
            todo += [
                (k.at[:, h * 256 : h * 256 + 128], ks.at[pl.ds(r + 512, 128), :]),
                (k.at[:, h * 256 + 128 : h * 256 + 256], vs.at[pl.ds(r + 512, 128), :]),
                (k.at[:, 512:640], ids.at[pl.ds(r + 512, 128), :]),
            ]
            rows = pl.ds(d * 128, 128)
            todo += [
                (pv.at[rows, h * 256 : h * 256 + 128], ks.at[pl.ds(r, 128), :]),
                (pv.at[rows, h * 256 + 128 : h * 256 + 256], vs.at[pl.ds(r, 128), :]),
                (pv.at[rows, 512:640], ids.at[pl.ds(r, 128), :]),
            ]
        run_copies(todo, sems)

        low = xh * 512
        own_ids = ids[512:1024, :].astype(F32)
        prev_ids = ids[0:512, :].astype(F32)
        second = xh.astype(F32)

        def count(top):
            a = jnp.sum(jnp.where(own_ids <= top, 1.0, 0.0), axis=0, keepdims=True)
            b = jnp.sum(jnp.where(prev_ids <= top, 1.0, 0.0), axis=0, keepdims=True)
            return (a + second * b)[:, 0:1].astype(jnp.int32)

        first, both = count(0.5), count(1.5)
        acck[...] = jnp.zeros_like(acck)
        accv[...] = jnp.zeros_like(accv)
        for blk in range(2):
            lo = blk * 256
            t = lax.broadcasted_iota(jnp.int32, (1, 256), 1) + lo
            ta = t + low
            start = jnp.where(ta < first, 0, jnp.where(ta < both, first, both)) - low
            u = lax.broadcasted_iota(jnp.int32, (768, 256), 0) + (lo - 512)
            bias[blk] = jnp.where((u <= t) & (u >= start), 0.0, NEG)

        def head(hq, _):
            cols = pl.ds(mult(hq, 128), 128)
            for blk in range(2):
                lo = blk * 256
                keys = ks[lo : lo + 768, :]
                vals = vs[lo : lo + 768, :]
                qq = qs[lo : lo + 256, cols]
                gg = gs[lo : lo + 256, cols]
                nt = (((1,), (1,)), ((), ()))
                sc = lax.dot_general(keys, qq, nt, preferred_element_type=F32) * SCALE + bias[blk]
                e = jnp.exp(sc - jnp.max(sc, axis=0, keepdims=True))
                p = e * (1.0 / jnp.sum(e, axis=0, keepdims=True))
                p_low = p.astype(BF16)
                dp = lax.dot_general(vals, gg, nt, preferred_element_type=F32)
                delta = jnp.sum(p_low.astype(F32) * dp, axis=0, keepdims=True)
                ds = (p * (dp - delta) * SCALE).astype(BF16)
                tn = (((0,), (0,)), ((), ()))
                dqt = lax.dot_general(keys, ds, tn, preferred_element_type=F32)
                dq[cols, lo : lo + 256] = dqt.astype(BF16)
                acck[lo : lo + 768, :] += jnp.dot(ds, qq, preferred_element_type=F32)
                accv[lo : lo + 768, :] += jnp.dot(p_low, gg, preferred_element_type=F32)
            return 0

        lax.fori_loop(0, 4, head, 0, unroll=4)
        dkv[0:128, :] = acck[512:1024, :].T
        dkv[128:256, :] = accv[512:1024, :].T
        dprev[0:128, :] = acck[0:512, :].astype(BF16).T
        dprev[128:256, :] = accv[0:512, :].astype(BF16).T

    return call(
        attention_body,
        [
            jax.ShapeDtypeStruct((512, 512), BF16),
            jax.ShapeDtypeStruct((256, 512), F32),
            jax.ShapeDtypeStruct((256, 512), BF16),
        ],
        [
            pltpu.VMEM((1024, 128), BF16),
            pltpu.VMEM((1024, 128), BF16),
            pltpu.VMEM((1024, 128), BF16),
            pltpu.VMEM((2, 768, 256), F32),
            pltpu.VMEM((1024, 128), F32),
            pltpu.VMEM((1024, 128), F32),
            pltpu.SemaphoreType.DMA((32,)),
        ],
        12 * 10**9,
        10**6,
        [VMEM] * 2 + [ANY] * 5,
        [VMEM] * 3,
    )(queries, grads, own, *keys, before)


def gather_a(gt):
    def gather_a_body(a0, b0, a1, b1, ga, sems):
        todo = []
        for h, pair in enumerate(((a0, b0), (a1, b1))):
            for i, src in enumerate(pair):
                to = ga.at[h * 384 : (h + 1) * 384, i * 512 : (i + 1) * 512]
                todo.append((src.at[0:384, :], to))
        run_copies(todo, sems)

    return call(
        gather_a_body,
        jax.ShapeDtypeStruct((768, 1024), BF16),
        [pltpu.SemaphoreType.DMA((4,))],
        10**8,
        10**6,
        [ANY] * 4,
        VMEM,
    )(*gt)


def gather_b(gt, kv):
    def gather_b_body(a0, b0, a1, b1, k, l, gb, sems):
        todo = []
        for h, pair in enumerate(((a0, b0), (a1, b1))):
            for i, (src, low) in enumerate(zip(pair, (k, l))):
                cols = slice(i * 512, (i + 1) * 512)
                todo += [
                    (src.at[384:512, :], gb.at[h * 384 : h * 384 + 128, cols]),
                    (low.at[h * 256 : (h + 1) * 256, :], gb.at[h * 384 + 128 : (h + 1) * 384, cols]),
                ]
        run_copies(todo, sems)

    return call(
        gather_b_body,
        jax.ShapeDtypeStruct((768, 1024), BF16),
        [pltpu.SemaphoreType.DMA((8,))],
        10**8,
        10**6,
        [ANY] * 6,
        VMEM,
    )(*gt, *kv)


def product(a, b):
    return jnp.dot(a, b, preferred_element_type=F32)


def z_cols(xs, z):
    return jnp.concatenate(
        [xs[:, pl.ds(mult(z, BW), BW)], xs[:, pl.ds(mult(z + 4, BW), BW)]], axis=1
    )


def far_a(ga, inputs):
    def far_a_body(g, own, r1, r3, r2a, r2b, xs, up, down, sems):
        here = place()
        y = here["y"]

        def at(d, half):
            row = lax.rem(y - d + 4, 4) * 128 + half * 512
            return xs.at[pl.ds(pl.multiple_of(row, 128), 128), :]

        todo = []
        for d, r in ((0, own), (1, r1), (3, r3)):
            todo += [(r.at[0:128, :], at(d, 0)), (r.at[128:256, :], at(d, 1))]
        run_copies(todo + [(r2a, at(2, 0)), (r2b, at(2, 1))], sems)
        p = product(g[...], z_cols(xs, lax.rem(here["z"] + 2, 4)))
        up[...] = p[:, 0:BW].astype(BF16)
        down[...] = p[:, BW:].astype(BF16)

    return call(
        far_a_body,
        [jax.ShapeDtypeStruct((1024, 8 * BW), BF16)] + [jax.ShapeDtypeStruct((768, BW), BF16)] * 2,
        [pltpu.SemaphoreType.DMA((8,))],
        10**9,
        10**6,
        [VMEM] + [ANY] * 5,
        [VMEM] * 3,
    )(ga, *inputs)


def x_product(g, xs, to, lo, size):
    cols = xs[:, pl.ds(mult(lax.rem(to, 2) * 4 + lo, BW), size * BW)]
    return product(g[pl.ds(mult(to // 2, 384), 384), :], cols)


def far_b(gb, xs):
    def far_b_body(g, x, up, down):
        to = lax.rem(place()["x"] + 2, 4)
        for o, lo in ((up, 0), (down, 2)):
            o[...] = x_product(g, x, to, lo, 2).astype(BF16)

    return call(
        far_b_body,
        [jax.ShapeDtypeStruct((384, 2 * BW), BF16)] * 2,
        [],
        10**9,
        10**6,
        [VMEM] * 2,
        [VMEM] * 2,
    )(gb, xs)


def near_a(ga, xs):
    def near_a_body(g, x, up, down, own):
        z = place()["z"]
        for o, d in ((up, 1), (down, 3), (own, 0)):
            o[...] = product(g[...], z_cols(x, lax.rem(z + d, 4)))

    return call(
        near_a_body,
        [jax.ShapeDtypeStruct((768, 2 * BW), F32)] * 3,
        [],
        10**9,
        10**6,
        [VMEM] * 2,
        [VMEM] * 3,
    )(ga, xs)


def near_b(gb, xs):
    def near_b_body(g, x, up, down, own):
        for o, d in ((up, 1), (down, 3), (own, 0)):
            o[...] = x_product(g, x, lax.rem(place()["x"] + d, 4), 0, 4)

    return call(
        near_b_body,
        [jax.ShapeDtypeStruct((384, 4 * BW), F32)] * 3,
        [],
        10**9,
        10**6,
        [VMEM] * 2,
        [VMEM] * 3,
    )(gb, xs)


def add_near(up, down, got_up, got_down):
    rows, cols = up.shape
    half = cols // 2

    def add_near_body(u, d, gu, gd, ou, od):
        ou[:, 0:half] = (u[:, 0:half] + gu[...].astype(F32)).astype(BF16)
        ou[:, half:] = u[:, half:].astype(BF16)
        od[:, 0:half] = d[:, 0:half].astype(BF16)
        od[:, half:] = (d[:, half:] + gd[...].astype(F32)).astype(BF16)

    return call(
        add_near_body,
        [jax.ShapeDtypeStruct((rows, cols), BF16)] * 2,
        [],
        5 * 10**8,
        10**6,
        [VMEM] * 4,
        [VMEM] * 2,
    )(up, down, got_up, got_down)


def partial_shapes(*shape):
    return [jax.ShapeDtypeStruct(shape, F32 if d == 0 else BF16) for d in range(4)]


def total(refs):
    t = refs[0][...]
    for r in refs[1:]:
        t = t + r[...].astype(F32)
    return t


def add_a(parts):
    def add_a_body(*refs):
        outs, t = refs[3:7], refs[7]
        x = place()["x"]
        t[...] = total(refs[0:3])
        for d in range(4):
            to = lax.rem(x + d, 4)
            rows, cols = pl.ds(mult(to // 2, 384), 384), pl.ds(mult(lax.rem(to, 2), BW), BW)
            outs[d][...] = t[rows, cols].astype(outs[d].dtype)

    return call(
        add_a_body,
        partial_shapes(384, 256),
        [pltpu.VMEM((768, 2 * BW), F32)],
        5 * 10**8,
        10**6,
        [VMEM] * 3,
        [VMEM] * 4,
    )(*parts)


def add_b(parts):
    def add_b_body(*refs):
        outs, t = refs[3:7], refs[7]
        z = place()["z"]
        t[...] = total(refs[0:3])
        for d in range(4):
            o = outs[d]
            o[...] = t[:, pl.ds(mult(lax.rem(z + d, 4), BW), BW)].astype(o.dtype)

    return call(
        add_b_body,
        partial_shapes(384, 256),
        [pltpu.VMEM((384, 4 * BW), F32)],
        5 * 10**8,
        10**6,
        [VMEM] * 3,
        [VMEM] * 4,
    )(*parts)


def finish(parts):
    def finish_body(*refs):
        qo, ko, vo = refs[8:]
        a = (total(refs[0:4]) * FACTOR).T
        b = (total(refs[4:8]) * FACTOR).T
        qo[:, 0:384] = a
        qo[:, 384:512] = b[:, 0:128]
        ko[...] = b[:, 128:256]
        vo[...] = b[:, 256:384]

    return call(
        finish_body,
        [
            jax.ShapeDtypeStruct((256, 512), F32),
            jax.ShapeDtypeStruct((256, 128), F32),
            jax.ShapeDtypeStruct((256, 128), F32),
        ],
        [],
        0,
        0,
        [VMEM] * 8,
        [VMEM] * 3,
    )(*parts)


def after(x, *deps):
    return lax.optimization_barrier((x, *deps))[0]


def ring(label, far, up, down, **axis):
    step = {k: -v for k, v in axis.items()}
    got_up = send(label + "_far_up", far[0], **axis)
    got_down = send(label + "_far_down", far[1], **step)
    ou, od = add_near(up, down, got_up, got_down)
    return send(label + "_up", ou, **axis), send(label + "_down", od, **step)


def per_device(hidden_in, queries, key_heads, saved_value_heads, out_grads, doc_ids):
    *kmsg, own, q01, q02, q03, q11, q12, q13 = pack_heads(
        queries, key_heads, saved_value_heads, out_grads, doc_ids
    )
    keys = [send("keys_y%d" % (d + 1), m, dy=d + 1) for d, m in enumerate(kmsg)]
    keep, give = pack_inputs(after(hidden_in, own))
    got = send("swap_inputs", give, dc=1)
    a1 = send("queries0_y1", q01, dy=1)
    a3 = send("queries0_y3", q03, dy=3)
    a2 = send("queries0_y2", q02, dy=2)
    before = send("half", jnp.concatenate([own] + keys, axis=0), dx=2)
    b1 = send("queries1_y1", after(q11, a1), dy=1)
    b3 = send("queries1_y3", after(q13, a1), dy=3)
    b2 = send("queries1_y2", after(q12, a1, a3), dy=2)
    sent = after(jnp.concatenate([keep, got], axis=0), a1, a2, a3)
    up = send("inputs_up", sent, dy=1)
    down = send("inputs_down", sent, dy=-1)

    def attend(h, dep, msgs):
        qs, gs = arrange(h, after(queries, *dep), out_grads, msgs)
        return attention(h, qs, gs, own, keys, before)

    dq0, dkv0, back0 = attend(0, (), (a1, a2, a3))
    swap0 = send("swap_dq0", dq0, dc=1)
    dq1, dkv1, back1 = attend(1, (dq0,), (b1, b2, b3))
    fwd = send("inputs_up2", after(up[0:128], dq1), dy=1)
    rev = send("inputs_down2", after(down[128:256], dq1), dy=-1)
    swap1 = send("swap_dq1", dq1, dc=1)
    ret = send("back", jnp.concatenate([back0, back1], axis=0), dx=2)
    ret = after(ret, fwd, rev, swap1).astype(F32)
    low = (jnp.concatenate([dkv0, dkv1], axis=0) + ret).astype(BF16)
    kv = (low, send("swap_dkv", low, dc=1))
    inputs = (sent, up, down, fwd, rev)
    gt = (dq0, swap0, dq1, swap1)

    ga = gather_a(gt)
    xs, *fa = far_a(ga, inputs)
    gb = gather_b(gt, kv)
    fb = far_b(after(gb, fa[0]), xs)
    ua, da, oa = near_a(after(ga, fb[0]), xs)
    ub, db, ob = near_b(after(gb, oa), xs)
    ra = ring("reduce_a", fa, ua, da, dz=1)
    rb = ring("reduce_b", fb, ub, db, dx=1)
    ma = add_a([oa, *ra])
    sa = [send("second_a_x%d" % d, ma[d], dx=d) for d in (1, 3, 2)]
    mb = add_b([ob, *rb])
    sb = [send("second_b_z%d" % d, mb[d], dz=d) for d in (1, 3, 2)]
    return finish([ma[0], *sa, mb[0], *sb])


def solution(mesh):
    return jax.shard_map(
        per_device,
        mesh=mesh,
        in_specs=(
            P("grp", "sp", None),
            P("grp", "sp", None),
            P("grp", "sp", None),
            P("grp", "sp", None),
            P("grp", "sp", None),
            P("grp", "sp"),
        ),
        out_specs=(P("grp", "sp"), P("grp", "sp"), P("grp", "sp")),
        check_vma=False,
    )
```

```python
import math

import jax
import jax.numpy as jnp
from jax import lax
from jax.experimental import pallas as pl
from jax.experimental.pallas import tpu as pltpu
from jax.sharding import PartitionSpec as P

HEAD = 128
NEG = -1e30
SCALE = 1.0 / math.sqrt(HEAD)
FACTOR = 16384 ** -0.5
BW = 256
VM = 32 * 1024 * 1024
BIG = 60 * 1024 * 1024
F32 = jnp.float32
BF16 = jnp.bfloat16
ANY = pl.BlockSpec(memory_space=pl.ANY)
VMEM = pl.BlockSpec(memory_space=pltpu.VMEM)


def place():
    g = lax.axis_index("grp")
    s = lax.axis_index("sp")
    return dict(
        z=g // 4, x=(s // 4) * 2 + (g // 2) % 2, c=lax.rem(g, 2), y=lax.rem(s, 4), xh=s // 4
    )


def pairs(dx=0, dy=0, dz=0, dc=0, only_half=None):
    out = []
    for z in range(4):
        for x in range(4):
            for y in range(4):
                for c in range(2):
                    if only_half is not None and x // 2 != only_half:
                        continue

                    def flat(z, x, y, c):
                        return (z * 4 + (x % 2) * 2 + c) * 8 + (x // 2) * 4 + y

                    out.append(
                        (
                            flat(z, x, y, c),
                            flat((z + dz) % 4, (x + dx) % 4, (y + dy) % 4, (c + dc) % 2),
                        )
                    )
    return out


def send(label, a, **k):
    with jax.named_scope(label):
        return lax.ppermute(a, ("grp", "sp"), pairs(**k))


def call(body, outs, scratch, flops, nbytes, in_specs, out_specs, vm=VM):
    return pl.pallas_call(
        body,
        name=body.__name__,
        out_shape=outs,
        in_specs=in_specs,
        out_specs=out_specs,
        scratch_shapes=scratch,
        compiler_params=pltpu.CompilerParams(vmem_limit_bytes=vm),
        cost_estimate=pl.CostEstimate(flops=flops, bytes_accessed=nbytes, transcendentals=0),
    )


def start_copies(todo, sems):
    made = [pltpu.make_async_copy(a, b, sems.at[i]) for i, (a, b) in enumerate(todo)]
    for m in made:
        m.start()
    return made


def run_copies(todo, sems):
    for m in start_copies(todo, sems):
        m.wait()


def mult(i, n):
    return pl.multiple_of(i * n, n)


def pack_keys(keys, values, ids):
    def pack_keys_body(k, v, i, k1, k2, k3, k0, sems):
        y = place()["y"]
        todo = []
        for d, o in ((1, k1), (3, k3), (2, k2), (0, k0)):
            for h in range(2):
                cols = pl.ds(mult(h * 4 + lax.rem(y + d, 4), 128), 128)
                todo += [
                    (k.at[0, :, cols], o.at[:, h * 256 : h * 256 + 128]),
                    (v.at[0, :, cols], o.at[:, h * 256 + 128 : h * 256 + 256]),
                ]
        made = start_copies(todo, sems)
        spread = jnp.broadcast_to(i[...].astype(F32), (128, 128)).T.astype(BF16)
        for o in (k1, k2, k3, k0):
            o[:, 512:640] = spread
        for m in made:
            m.wait()

    return call(
        pack_keys_body,
        [jax.ShapeDtypeStruct((128, 640), BF16)] * 4,
        [pltpu.SemaphoreType.DMA((16,))],
        10**8,
        10**6,
        [ANY] * 2 + [VMEM],
        [VMEM] * 4,
        BIG,
    )(keys, values, ids)


def pack_queries(queries, grads):
    def pack_queries_body(q, g, *refs):
        outs, sems = refs[:6], refs[6]
        y = place()["y"]
        todo = []
        for h in range(2):
            for d in (1, 2, 3):
                o = outs[h * 3 + d - 1]
                cols = pl.ds(mult(h * 4 + lax.rem(y + d, 4), 512), 512)
                todo += [(q.at[0, :, cols], o.at[:, 0:512]), (g.at[0, :, cols], o.at[:, 512:1024])]
        run_copies(todo, sems)

    return call(
        pack_queries_body,
        [jax.ShapeDtypeStruct((128, 1024), BF16)] * 6,
        [pltpu.SemaphoreType.DMA((12,))],
        10**8,
        10**6,
        [ANY] * 2,
        [VMEM] * 6,
        BIG,
    )(queries, grads)


def pack_inputs(hidden):
    def pack_inputs_body(x, keep, give, sems):
        c = place()["c"]
        todo = []
        for b in range(8):
            at = (b % 2) * 4 + b // 2
            for o, cc in ((keep, c), (give, 1 - c)):
                cols = pl.ds(mult(b * 2 + cc, BW), BW)
                todo.append((x.at[0, :, cols], o.at[:, at * BW : (at + 1) * BW]))
        run_copies(todo, sems)

    shape = jax.ShapeDtypeStruct((128, 8 * BW), BF16)
    return call(
        pack_inputs_body,
        [shape] * 2,
        [pltpu.SemaphoreType.DMA((16,))],
        10**9,
        10**6,
        [ANY],
        [VMEM] * 2,
        BIG,
    )(hidden)


def arrange(h, queries, grads, msgs):
    def arrange_body(q, g, q1, q2, q3, qs, gs, sems):
        y = place()["y"]
        cols, row = pl.ds(mult(h * 4 + y, 512), 512), pl.ds(mult(y, 128), 128)
        todo = [(q.at[0, :, cols], qs.at[row, :]), (g.at[0, :, cols], gs.at[row, :])]
        for d, m in ((1, q1), (2, q2), (3, q3)):
            row = pl.ds(mult(lax.rem(y - d + 4, 4), 128), 128)
            todo += [(m.at[:, 0:512], qs.at[row, :]), (m.at[:, 512:1024], gs.at[row, :])]
        run_copies(todo, sems)

    return call(
        arrange_body,
        [jax.ShapeDtypeStruct((512, 512), BF16)] * 2,
        [pltpu.SemaphoreType.DMA((8,))],
        6 * 10**9,
        10**6,
        [ANY] * 5,
        [VMEM] * 2,
    )(queries, grads, *msgs)


def attention(h, queries, grads, own, keys, before):
    def attention_body(qs, gs, kv, k1, k2, k3, pv, dq, dkv, dprev, ks, vs, ids, bias, acck, accv, sems):
        here = place()
        y, xh = here["y"], here["xh"]
        todo = []
        for d, k in ((0, kv), (1, k1), (2, k2), (3, k3)):
            r = mult(lax.rem(y - d + 4, 4), 128)
            todo += [
                (k.at[:, h * 256 : h * 256 + 128], ks.at[pl.ds(r + 512, 128), :]),
                (k.at[:, h * 256 + 128 : h * 256 + 256], vs.at[pl.ds(r + 512, 128), :]),
                (k.at[:, 512:640], ids.at[pl.ds(r + 512, 128), :]),
            ]
            rows = pl.ds(d * 128, 128)
            todo += [
                (pv.at[rows, h * 256 : h * 256 + 128], ks.at[pl.ds(r, 128), :]),
                (pv.at[rows, h * 256 + 128 : h * 256 + 256], vs.at[pl.ds(r, 128), :]),
                (pv.at[rows, 512:640], ids.at[pl.ds(r, 128), :]),
            ]
        run_copies(todo, sems)

        low = xh * 512
        own_ids = ids[512:1024, :].astype(F32)
        prev_ids = ids[0:512, :].astype(F32)
        second = xh.astype(F32)

        def count(top):
            a = jnp.sum(jnp.where(own_ids <= top, 1.0, 0.0), axis=0, keepdims=True)
            b = jnp.sum(jnp.where(prev_ids <= top, 1.0, 0.0), axis=0, keepdims=True)
            return (a + second * b)[:, 0:1].astype(jnp.int32)

        first, both = count(0.5), count(1.5)
        acck[...] = jnp.zeros_like(acck)
        accv[...] = jnp.zeros_like(accv)
        for blk in range(2):
            lo = blk * 256
            t = lax.broadcasted_iota(jnp.int32, (1, 256), 1) + lo
            ta = t + low
            start = jnp.where(ta < first, 0, jnp.where(ta < both, first, both)) - low
            u = lax.broadcasted_iota(jnp.int32, (768, 256), 0) + (lo - 512)
            bias[blk] = jnp.where((u <= t) & (u >= start), 0.0, NEG)

        def head(hq, _):
            cols = pl.ds(mult(hq, 128), 128)
            for blk in range(2):
                lo = blk * 256
                keys = ks[lo : lo + 768, :]
                vals = vs[lo : lo + 768, :]
                qq = qs[lo : lo + 256, cols]
                gg = gs[lo : lo + 256, cols]
                nt = (((1,), (1,)), ((), ()))
                sc = lax.dot_general(keys, qq, nt, preferred_element_type=F32) * SCALE + bias[blk]
                e = jnp.exp(sc - jnp.max(sc, axis=0, keepdims=True))
                p = e * (1.0 / jnp.sum(e, axis=0, keepdims=True))
                p_low = p.astype(BF16)
                dp = lax.dot_general(vals, gg, nt, preferred_element_type=F32)
                delta = jnp.sum(p_low.astype(F32) * dp, axis=0, keepdims=True)
                ds = (p * (dp - delta) * SCALE).astype(BF16)
                tn = (((0,), (0,)), ((), ()))
                dqt = lax.dot_general(keys, ds, tn, preferred_element_type=F32)
                dq[cols, lo : lo + 256] = dqt.astype(BF16)
                acck[lo : lo + 768, :] += jnp.dot(ds, qq, preferred_element_type=F32)
                accv[lo : lo + 768, :] += jnp.dot(p_low, gg, preferred_element_type=F32)
            return 0

        lax.fori_loop(0, 4, head, 0, unroll=4)
        dkv[0:128, :] = acck[512:1024, :].T
        dkv[128:256, :] = accv[512:1024, :].T
        dprev[0:128, :] = acck[0:512, :].astype(BF16).T
        dprev[128:256, :] = accv[0:512, :].astype(BF16).T

    return call(
        attention_body,
        [
            jax.ShapeDtypeStruct((512, 512), BF16),
            jax.ShapeDtypeStruct((256, 512), F32),
            jax.ShapeDtypeStruct((256, 512), BF16),
        ],
        [
            pltpu.VMEM((1024, 128), BF16),
            pltpu.VMEM((1024, 128), BF16),
            pltpu.VMEM((1024, 128), BF16),
            pltpu.VMEM((2, 768, 256), F32),
            pltpu.VMEM((1024, 128), F32),
            pltpu.VMEM((1024, 128), F32),
            pltpu.SemaphoreType.DMA((32,)),
        ],
        12 * 10**9,
        10**6,
        [VMEM] * 2 + [ANY] * 5,
        [VMEM] * 3,
    )(queries, grads, own, *keys, before)


def gather_a(gt):
    def gather_a_body(a0, b0, a1, b1, ga, sems):
        todo = []
        for h, pair in enumerate(((a0, b0), (a1, b1))):
            for i, src in enumerate(pair):
                to = ga.at[h * 384 : (h + 1) * 384, i * 512 : (i + 1) * 512]
                todo.append((src.at[0:384, :], to))
        run_copies(todo, sems)

    return call(
        gather_a_body,
        jax.ShapeDtypeStruct((768, 1024), BF16),
        [pltpu.SemaphoreType.DMA((4,))],
        10**8,
        10**6,
        [ANY] * 4,
        VMEM,
    )(*gt)


def gather_b(gt, kv):
    def gather_b_body(a0, b0, a1, b1, k, l, gb, sems):
        todo = []
        for h, pair in enumerate(((a0, b0), (a1, b1))):
            for i, (src, low) in enumerate(zip(pair, (k, l))):
                cols = slice(i * 512, (i + 1) * 512)
                todo += [
                    (src.at[384:512, :], gb.at[h * 384 : h * 384 + 128, cols]),
                    (low.at[h * 256 : (h + 1) * 256, :], gb.at[h * 384 + 128 : (h + 1) * 384, cols]),
                ]
        run_copies(todo, sems)

    return call(
        gather_b_body,
        jax.ShapeDtypeStruct((768, 1024), BF16),
        [pltpu.SemaphoreType.DMA((8,))],
        10**8,
        10**6,
        [ANY] * 6,
        VMEM,
    )(*gt, *kv)


def product(a, b):
    return jnp.dot(a, b, preferred_element_type=F32)


def z_cols(xs, z):
    return jnp.concatenate(
        [xs[:, pl.ds(mult(z, BW), BW)], xs[:, pl.ds(mult(z + 4, BW), BW)]], axis=1
    )


def far_a(ga, inputs):
    def far_a_body(g, own, r1, r3, r2a, r2b, xs, up, down, sems):
        here = place()
        y = here["y"]

        def at(d, half):
            row = lax.rem(y - d + 4, 4) * 128 + half * 512
            return xs.at[pl.ds(pl.multiple_of(row, 128), 128), :]

        todo = []
        for d, r in ((0, own), (1, r1), (3, r3)):
            todo += [(r.at[0:128, :], at(d, 0)), (r.at[128:256, :], at(d, 1))]
        run_copies(todo + [(r2a, at(2, 0)), (r2b, at(2, 1))], sems)
        p = product(g[...], z_cols(xs, lax.rem(here["z"] + 2, 4)))
        up[...] = p[:, 0:BW].astype(BF16)
        down[...] = p[:, BW:].astype(BF16)

    return call(
        far_a_body,
        [jax.ShapeDtypeStruct((1024, 8 * BW), BF16)] + [jax.ShapeDtypeStruct((768, BW), BF16)] * 2,
        [pltpu.SemaphoreType.DMA((8,))],
        10**9,
        10**6,
        [VMEM] + [ANY] * 5,
        [VMEM] * 3,
    )(ga, *inputs)


def x_product(g, xs, to, lo, size):
    cols = xs[:, pl.ds(mult(lax.rem(to, 2) * 4 + lo, BW), size * BW)]
    return product(g[pl.ds(mult(to // 2, 384), 384), :], cols)


def far_b(gb, xs):
    def far_b_body(g, x, up, down):
        to = lax.rem(place()["x"] + 2, 4)
        for o, lo in ((up, 0), (down, 2)):
            o[...] = x_product(g, x, to, lo, 2).astype(BF16)

    return call(
        far_b_body,
        [jax.ShapeDtypeStruct((384, 2 * BW), BF16)] * 2,
        [],
        10**9,
        10**6,
        [VMEM] * 2,
        [VMEM] * 2,
    )(gb, xs)


def near_a(ga, xs):
    def near_a_body(g, x, up, down, own):
        z = place()["z"]
        for o, d in ((up, 1), (down, 3), (own, 0)):
            o[...] = product(g[...], z_cols(x, lax.rem(z + d, 4)))

    return call(
        near_a_body,
        [jax.ShapeDtypeStruct((768, 2 * BW), F32)] * 3,
        [],
        10**9,
        10**6,
        [VMEM] * 2,
        [VMEM] * 3,
    )(ga, xs)


def near_b(gb, xs):
    def near_b_body(g, x, up, down, own):
        for o, d in ((up, 1), (down, 3), (own, 0)):
            o[...] = x_product(g, x, lax.rem(place()["x"] + d, 4), 0, 4)

    return call(
        near_b_body,
        [jax.ShapeDtypeStruct((384, 4 * BW), F32)] * 3,
        [],
        10**9,
        10**6,
        [VMEM] * 2,
        [VMEM] * 3,
    )(gb, xs)


def add_near(up, down, got_up, got_down):
    rows, cols = up.shape
    half = cols // 2

    def add_near_body(u, d, gu, gd, ou, od):
        ou[:, 0:half] = (u[:, 0:half] + gu[...].astype(F32)).astype(BF16)
        ou[:, half:] = u[:, half:].astype(BF16)
        od[:, 0:half] = d[:, 0:half].astype(BF16)
        od[:, half:] = (d[:, half:] + gd[...].astype(F32)).astype(BF16)

    return call(
        add_near_body,
        [jax.ShapeDtypeStruct((rows, cols), BF16)] * 2,
        [],
        5 * 10**8,
        10**6,
        [VMEM] * 4,
        [VMEM] * 2,
    )(up, down, got_up, got_down)


def partial_shapes(*shape):
    return [jax.ShapeDtypeStruct(shape, F32 if d == 0 else BF16) for d in range(4)]


def total(refs):
    t = refs[0][...]
    for r in refs[1:]:
        t = t + r[...].astype(F32)
    return t


def add_a(parts):
    def add_a_body(*refs):
        outs, t = refs[3:7], refs[7]
        x = place()["x"]
        t[...] = total(refs[0:3])
        for d in range(4):
            to = lax.rem(x + d, 4)
            rows, cols = pl.ds(mult(to // 2, 384), 384), pl.ds(mult(lax.rem(to, 2), BW), BW)
            outs[d][...] = t[rows, cols].astype(outs[d].dtype)

    return call(
        add_a_body,
        partial_shapes(384, 256),
        [pltpu.VMEM((768, 2 * BW), F32)],
        5 * 10**8,
        10**6,
        [VMEM] * 3,
        [VMEM] * 4,
    )(*parts)


def add_b(parts):
    def add_b_body(*refs):
        outs, t = refs[3:7], refs[7]
        z = place()["z"]
        t[...] = total(refs[0:3])
        for d in range(4):
            o = outs[d]
            o[...] = t[:, pl.ds(mult(lax.rem(z + d, 4), BW), BW)].astype(o.dtype)

    return call(
        add_b_body,
        partial_shapes(384, 256),
        [pltpu.VMEM((384, 4 * BW), F32)],
        5 * 10**8,
        10**6,
        [VMEM] * 3,
        [VMEM] * 4,
    )(*parts)


def finish(parts):
    def finish_body(*refs):
        qo, ko, vo = refs[8:]
        a = (total(refs[0:4]) * FACTOR).T
        b = (total(refs[4:8]) * FACTOR).T
        qo[:, 0:384] = a
        qo[:, 384:512] = b[:, 0:128]
        ko[...] = b[:, 128:256]
        vo[...] = b[:, 256:384]

    return call(
        finish_body,
        [
            jax.ShapeDtypeStruct((256, 512), F32),
            jax.ShapeDtypeStruct((256, 128), F32),
            jax.ShapeDtypeStruct((256, 128), F32),
        ],
        [],
        0,
        0,
        [VMEM] * 8,
        [VMEM] * 3,
    )(*parts)


def after(x, *deps):
    return lax.optimization_barrier((x, *deps))[0]


def ring(label, far, up, down, **axis):
    step = {k: -v for k, v in axis.items()}
    got_up = send(label + "_far_up", far[0], **axis)
    got_down = send(label + "_far_down", far[1], **step)
    ou, od = add_near(up, down, got_up, got_down)
    return send(label + "_up", ou, **axis), send(label + "_down", od, **step)


def per_device(hidden_in, queries, key_heads, saved_value_heads, out_grads, doc_ids):
    *kmsg, own = pack_keys(key_heads, saved_value_heads, doc_ids)
    q01, q02, q03, q11, q12, q13 = pack_queries(after(queries, own), out_grads)
    keys = [send("keys_y%d" % (d + 1), m, dy=d + 1) for d, m in enumerate(kmsg)]
    keep, give = pack_inputs(after(hidden_in, own))
    got = send("swap_inputs", give, dc=1)
    a1 = send("queries0_y1", q01, dy=1)
    a3 = send("queries0_y3", q03, dy=3)
    a2 = send("queries0_y2", q02, dy=2)
    before = send("half", jnp.concatenate([own] + keys, axis=0), dx=2)
    b1 = send("queries1_y1", after(q11, a1), dy=1)
    b3 = send("queries1_y3", after(q13, a1), dy=3)
    b2 = send("queries1_y2", after(q12, a1, a3), dy=2)
    sent = after(jnp.concatenate([keep, got], axis=0), a1, a2, a3)
    up = send("inputs_up", sent, dy=1)
    down = send("inputs_down", sent, dy=-1)

    def attend(h, dep, msgs):
        qs, gs = arrange(h, after(queries, *dep), out_grads, msgs)
        return attention(h, qs, gs, own, keys, before)

    dq0, dkv0, back0 = attend(0, (), (a1, a2, a3))
    swap0 = send("swap_dq0", dq0, dc=1)
    dq1, dkv1, back1 = attend(1, (dq0,), (b1, b2, b3))
    fwd = send("inputs_up2", after(up[0:128], dq1), dy=1)
    rev = send("inputs_down2", after(down[128:256], dq1), dy=-1)
    swap1 = send("swap_dq1", dq1, dc=1)
    ret = send("back", jnp.concatenate([back0, back1], axis=0), dx=2)
    ret = after(ret, fwd, rev, swap1).astype(F32)
    low = (jnp.concatenate([dkv0, dkv1], axis=0) + ret).astype(BF16)
    kv = (low, send("swap_dkv", low, dc=1))
    inputs = (sent, up, down, fwd, rev)
    gt = (dq0, swap0, dq1, swap1)

    ga = gather_a(gt)
    xs, *fa = far_a(ga, inputs)
    gb = gather_b(gt, kv)
    fb = far_b(after(gb, fa[0]), xs)
    ua, da, oa = near_a(after(ga, fb[0]), xs)
    ub, db, ob = near_b(after(gb, oa), xs)
    ra = ring("reduce_a", fa, ua, da, dz=1)
    rb = ring("reduce_b", fb, ub, db, dx=1)
    ma = add_a([oa, *ra])
    sa = [send("second_a_x%d" % d, ma[d], dx=d) for d in (1, 3, 2)]
    mb = add_b([ob, *rb])
    sb = [send("second_b_z%d" % d, mb[d], dz=d) for d in (1, 3, 2)]
    return finish([ma[0], *sa, mb[0], *sb])


def solution(mesh):
    return jax.shard_map(
        per_device,
        mesh=mesh,
        in_specs=(
            P("grp", "sp", None),
            P("grp", "sp", None),
            P("grp", "sp", None),
            P("grp", "sp", None),
            P("grp", "sp", None),
            P("grp", "sp"),
        ),
        out_specs=(P("grp", "sp"), P("grp", "sp"), P("grp", "sp")),
        check_vma=False,
    )
```

```python
import math

import jax
import jax.numpy as jnp
from jax import lax
from jax.experimental import pallas as pl
from jax.experimental.pallas import tpu as pltpu
from jax.sharding import PartitionSpec as P

HEAD = 128
NEG = -1e30
SCALE = 1.0 / math.sqrt(HEAD)
FACTOR = 16384 ** -0.5
BW = 256
VM = 32 * 1024 * 1024
BIG = 60 * 1024 * 1024
F32 = jnp.float32
BF16 = jnp.bfloat16
ANY = pl.BlockSpec(memory_space=pl.ANY)
VMEM = pl.BlockSpec(memory_space=pltpu.VMEM)


def place():
    g = lax.axis_index("grp")
    s = lax.axis_index("sp")
    return dict(
        z=g // 4, x=(s // 4) * 2 + (g // 2) % 2, c=lax.rem(g, 2), y=lax.rem(s, 4), xh=s // 4
    )


def pairs(dx=0, dy=0, dz=0, dc=0, only_half=None):
    out = []
    for z in range(4):
        for x in range(4):
            for y in range(4):
                for c in range(2):
                    if only_half is not None and x // 2 != only_half:
                        continue

                    def flat(z, x, y, c):
                        return (z * 4 + (x % 2) * 2 + c) * 8 + (x // 2) * 4 + y

                    out.append(
                        (
                            flat(z, x, y, c),
                            flat((z + dz) % 4, (x + dx) % 4, (y + dy) % 4, (c + dc) % 2),
                        )
                    )
    return out


def send(label, a, **k):
    with jax.named_scope(label):
        return lax.ppermute(a, ("grp", "sp"), pairs(**k))


def call(body, outs, scratch, flops, nbytes, in_specs, out_specs, vm=VM):
    return pl.pallas_call(
        body,
        name=body.__name__,
        out_shape=outs,
        in_specs=in_specs,
        out_specs=out_specs,
        scratch_shapes=scratch,
        compiler_params=pltpu.CompilerParams(vmem_limit_bytes=vm),
        cost_estimate=pl.CostEstimate(flops=flops, bytes_accessed=nbytes, transcendentals=0),
    )


def start_copies(todo, sems):
    made = [pltpu.make_async_copy(a, b, sems.at[i]) for i, (a, b) in enumerate(todo)]
    for m in made:
        m.start()
    return made


def run_copies(todo, sems):
    for m in start_copies(todo, sems):
        m.wait()


def mult(i, n):
    return pl.multiple_of(i * n, n)


def pack_keys(keys, values, ids):
    def pack_keys_body(k, v, i, k1, k2, k3, k0, sems):
        y = place()["y"]
        todo = []
        for d, o in ((1, k1), (3, k3), (2, k2), (0, k0)):
            for h in range(2):
                cols = pl.ds(mult(h * 4 + lax.rem(y + d, 4), 128), 128)
                todo += [
                    (k.at[0, :, cols], o.at[0:128, h * 256 : h * 256 + 128]),
                    (v.at[0, :, cols], o.at[0:128, h * 256 + 128 : h * 256 + 256]),
                ]
        made = start_copies(todo, sems)
        spread = jnp.broadcast_to(i[...].astype(F32), (16, 128)).astype(BF16)
        for o in (k1, k2, k3, k0):
            for part in range(4):
                o[128:144, part * 128 : (part + 1) * 128] = spread
        for m in made:
            m.wait()

    return call(
        pack_keys_body,
        [jax.ShapeDtypeStruct((144, 512), BF16)] * 4,
        [pltpu.SemaphoreType.DMA((16,))],
        10**8,
        10**6,
        [ANY] * 2 + [VMEM],
        [VMEM] * 4,
        BIG,
    )(keys, values, ids)


def pack_queries(queries, grads):
    def pack_queries_body(q, g, *refs):
        outs, sems = refs[:6], refs[6]
        y = place()["y"]
        todo = []
        for h in range(2):
            for d in (1, 2, 3):
                o = outs[h * 3 + d - 1]
                cols = pl.ds(mult(h * 4 + lax.rem(y + d, 4), 512), 512)
                todo += [(q.at[0, :, cols], o.at[:, 0:512]), (g.at[0, :, cols], o.at[:, 512:1024])]
        run_copies(todo, sems)

    return call(
        pack_queries_body,
        [jax.ShapeDtypeStruct((128, 1024), BF16)] * 6,
        [pltpu.SemaphoreType.DMA((12,))],
        10**8,
        10**6,
        [ANY] * 2,
        [VMEM] * 6,
        BIG,
    )(queries, grads)


def pack_inputs(hidden):
    def pack_inputs_body(x, keep, give, sems):
        c = place()["c"]
        todo = []
        for b in range(8):
            at = (b % 2) * 4 + b // 2
            for o, cc in ((keep, c), (give, 1 - c)):
                cols = pl.ds(mult(b * 2 + cc, BW), BW)
                todo.append((x.at[0, :, cols], o.at[:, at * BW : (at + 1) * BW]))
        run_copies(todo, sems)

    shape = jax.ShapeDtypeStruct((128, 8 * BW), BF16)
    return call(
        pack_inputs_body,
        [shape] * 2,
        [pltpu.SemaphoreType.DMA((16,))],
        10**9,
        10**6,
        [ANY],
        [VMEM] * 2,
        BIG,
    )(hidden)


def arrange(h, queries, grads, msgs):
    def arrange_body(q, g, q1, q2, q3, qs, gs, sems):
        y = place()["y"]
        cols, row = pl.ds(mult(h * 4 + y, 512), 512), pl.ds(mult(y, 128), 128)
        todo = [(q.at[0, :, cols], qs.at[row, :]), (g.at[0, :, cols], gs.at[row, :])]
        for d, m in ((1, q1), (2, q2), (3, q3)):
            row = pl.ds(mult(lax.rem(y - d + 4, 4), 128), 128)
            todo += [(m.at[:, 0:512], qs.at[row, :]), (m.at[:, 512:1024], gs.at[row, :])]
        run_copies(todo, sems)

    return call(
        arrange_body,
        [jax.ShapeDtypeStruct((512, 512), BF16)] * 2,
        [pltpu.SemaphoreType.DMA((8,))],
        6 * 10**9,
        10**6,
        [ANY] * 5,
        [VMEM] * 2,
    )(queries, grads, *msgs)


def attention(h, queries, grads, own, keys, before):
    def attention_body(qs, gs, kv, k1, k2, k3, pv, dq, dkv, dprev, ks, vs, ids, bias, acck, accv, sems):
        here = place()
        y, xh = here["y"], here["xh"]
        todo = []
        for d, k in ((0, kv), (1, k1), (2, k2), (3, k3)):
            r = mult(lax.rem(y - d + 4, 4), 128)
            todo += [
                (k.at[0:128, h * 256 : h * 256 + 128], ks.at[pl.ds(r + 512, 128), :]),
                (k.at[0:128, h * 256 + 128 : h * 256 + 256], vs.at[pl.ds(r + 512, 128), :]),
                (k.at[128:144, 0:128], ids.at[d * 16 + 64 : d * 16 + 80, :]),
            ]
            lo = d * 144
            todo += [
                (pv.at[lo : lo + 128, h * 256 : h * 256 + 128], ks.at[pl.ds(r, 128), :]),
                (pv.at[lo : lo + 128, h * 256 + 128 : h * 256 + 256], vs.at[pl.ds(r, 128), :]),
                (pv.at[lo + 128 : lo + 144, 0:128], ids.at[d * 16 : d * 16 + 16, :]),
            ]
        run_copies(todo, sems)

        low = xh * 512
        own_ids = ids[64:128, :].astype(F32)
        prev_ids = ids[0:64, :].astype(F32)
        second = xh.astype(F32)

        def count(top):
            a = jnp.where(own_ids <= top, 1.0, 0.0)
            b = jnp.where(prev_ids <= top, 1.0, 0.0)
            each = jnp.sum(a + second * b, axis=1, keepdims=True)
            return (jnp.sum(each, axis=0, keepdims=True) * (1.0 / 16)).astype(jnp.int32)

        first, both = count(0.5), count(1.5)
        acck[...] = jnp.zeros_like(acck)
        accv[...] = jnp.zeros_like(accv)
        for blk in range(2):
            lo = blk * 256
            t = lax.broadcasted_iota(jnp.int32, (1, 256), 1) + lo
            ta = t + low
            start = jnp.where(ta < first, 0, jnp.where(ta < both, first, both)) - low
            u = lax.broadcasted_iota(jnp.int32, (768, 256), 0) + (lo - 512)
            bias[blk] = jnp.where((u <= t) & (u >= start), 0.0, NEG)

        def head(hq, _):
            cols = pl.ds(mult(hq, 128), 128)
            for blk in range(2):
                lo = blk * 256
                keys = ks[lo : lo + 768, :]
                vals = vs[lo : lo + 768, :]
                qq = qs[lo : lo + 256, cols]
                gg = gs[lo : lo + 256, cols]
                nt = (((1,), (1,)), ((), ()))
                sc = lax.dot_general(keys, qq, nt, preferred_element_type=F32) * SCALE + bias[blk]
                e = jnp.exp(sc - jnp.max(sc, axis=0, keepdims=True))
                p = e * (1.0 / jnp.sum(e, axis=0, keepdims=True))
                p_low = p.astype(BF16)
                dp = lax.dot_general(vals, gg, nt, preferred_element_type=F32)
                delta = jnp.sum(p_low.astype(F32) * dp, axis=0, keepdims=True)
                ds = (p * (dp - delta) * SCALE).astype(BF16)
                tn = (((0,), (0,)), ((), ()))
                dqt = lax.dot_general(keys, ds, tn, preferred_element_type=F32)
                dq[cols, lo : lo + 256] = dqt.astype(BF16)
                acck[lo : lo + 768, :] += jnp.dot(ds, qq, preferred_element_type=F32)
                accv[lo : lo + 768, :] += jnp.dot(p_low, gg, preferred_element_type=F32)
            return 0

        lax.fori_loop(0, 4, head, 0, unroll=4)
        dkv[0:128, :] = acck[512:1024, :].T
        dkv[128:256, :] = accv[512:1024, :].T
        dprev[0:128, :] = acck[0:512, :].astype(BF16).T
        dprev[128:256, :] = accv[0:512, :].astype(BF16).T

    return call(
        attention_body,
        [
            jax.ShapeDtypeStruct((512, 512), BF16),
            jax.ShapeDtypeStruct((256, 512), F32),
            jax.ShapeDtypeStruct((256, 512), BF16),
        ],
        [
            pltpu.VMEM((1024, 128), BF16),
            pltpu.VMEM((1024, 128), BF16),
            pltpu.VMEM((128, 128), BF16),
            pltpu.VMEM((2, 768, 256), F32),
            pltpu.VMEM((1024, 128), F32),
            pltpu.VMEM((1024, 128), F32),
            pltpu.SemaphoreType.DMA((32,)),
        ],
        12 * 10**9,
        10**6,
        [VMEM] * 2 + [ANY] * 5,
        [VMEM] * 3,
    )(queries, grads, own, *keys, before)


def gather_a(gt):
    def gather_a_body(a0, b0, a1, b1, ga, sems):
        todo = []
        for h, pair in enumerate(((a0, b0), (a1, b1))):
            for i, src in enumerate(pair):
                to = ga.at[h * 384 : (h + 1) * 384, i * 512 : (i + 1) * 512]
                todo.append((src.at[0:384, :], to))
        run_copies(todo, sems)

    return call(
        gather_a_body,
        jax.ShapeDtypeStruct((768, 1024), BF16),
        [pltpu.SemaphoreType.DMA((4,))],
        10**8,
        10**6,
        [ANY] * 4,
        VMEM,
    )(*gt)


def gather_b(gt, kv):
    def gather_b_body(a0, b0, a1, b1, k, l, gb, sems):
        todo = []
        for h, pair in enumerate(((a0, b0), (a1, b1))):
            for i, (src, low) in enumerate(zip(pair, (k, l))):
                cols = slice(i * 512, (i + 1) * 512)
                todo += [
                    (src.at[384:512, :], gb.at[h * 384 : h * 384 + 128, cols]),
                    (low.at[h * 256 : (h + 1) * 256, :], gb.at[h * 384 + 128 : (h + 1) * 384, cols]),
                ]
        run_copies(todo, sems)

    return call(
        gather_b_body,
        jax.ShapeDtypeStruct((768, 1024), BF16),
        [pltpu.SemaphoreType.DMA((8,))],
        10**8,
        10**6,
        [ANY] * 6,
        VMEM,
    )(*gt, *kv)


def product(a, b):
    return jnp.dot(a, b, preferred_element_type=F32)


def z_cols(xs, z):
    return jnp.concatenate(
        [xs[:, pl.ds(mult(z, BW), BW)], xs[:, pl.ds(mult(z + 4, BW), BW)]], axis=1
    )


def far_a(ga, inputs):
    def far_a_body(g, own, r1, r3, r2a, r2b, xs, up, down, sems):
        here = place()
        y = here["y"]

        def at(d, half):
            row = lax.rem(y - d + 4, 4) * 128 + half * 512
            return xs.at[pl.ds(pl.multiple_of(row, 128), 128), :]

        todo = []
        for d, r in ((0, own), (1, r1), (3, r3)):
            todo += [(r.at[0:128, :], at(d, 0)), (r.at[128:256, :], at(d, 1))]
        run_copies(todo + [(r2a, at(2, 0)), (r2b, at(2, 1))], sems)
        p = product(g[...], z_cols(xs, lax.rem(here["z"] + 2, 4)))
        up[...] = p[:, 0:BW].astype(BF16)
        down[...] = p[:, BW:].astype(BF16)

    return call(
        far_a_body,
        [jax.ShapeDtypeStruct((1024, 8 * BW), BF16)] + [jax.ShapeDtypeStruct((768, BW), BF16)] * 2,
        [pltpu.SemaphoreType.DMA((8,))],
        10**9,
        10**6,
        [VMEM] + [ANY] * 5,
        [VMEM] * 3,
    )(ga, *inputs)


def x_product(g, xs, to, lo, size):
    cols = xs[:, pl.ds(mult(lax.rem(to, 2) * 4 + lo, BW), size * BW)]
    return product(g[pl.ds(mult(to // 2, 384), 384), :], cols)


def far_b(gb, xs):
    def far_b_body(g, x, up, down):
        to = lax.rem(place()["x"] + 2, 4)
        for o, lo in ((up, 0), (down, 2)):
            o[...] = x_product(g, x, to, lo, 2).astype(BF16)

    return call(
        far_b_body,
        [jax.ShapeDtypeStruct((384, 2 * BW), BF16)] * 2,
        [],
        10**9,
        10**6,
        [VMEM] * 2,
        [VMEM] * 2,
    )(gb, xs)


def near_a(ga, xs):
    def near_a_body(g, x, up, down, own):
        z = place()["z"]
        for o, d in ((up, 1), (down, 3), (own, 0)):
            o[...] = product(g[...], z_cols(x, lax.rem(z + d, 4)))

    return call(
        near_a_body,
        [jax.ShapeDtypeStruct((768, 2 * BW), F32)] * 3,
        [],
        10**9,
        10**6,
        [VMEM] * 2,
        [VMEM] * 3,
    )(ga, xs)


def near_b(gb, xs):
    def near_b_body(g, x, up, down, own):
        for o, d in ((up, 1), (down, 3), (own, 0)):
            o[...] = x_product(g, x, lax.rem(place()["x"] + d, 4), 0, 4)

    return call(
        near_b_body,
        [jax.ShapeDtypeStruct((384, 4 * BW), F32)] * 3,
        [],
        10**9,
        10**6,
        [VMEM] * 2,
        [VMEM] * 3,
    )(gb, xs)


def add_near(up, down, got_up, got_down):
    rows, cols = up.shape
    half = cols // 2

    def add_near_body(u, d, gu, gd, ou, od):
        ou[:, 0:half] = (u[:, 0:half] + gu[...].astype(F32)).astype(BF16)
        ou[:, half:] = u[:, half:].astype(BF16)
        od[:, 0:half] = d[:, 0:half].astype(BF16)
        od[:, half:] = (d[:, half:] + gd[...].astype(F32)).astype(BF16)

    return call(
        add_near_body,
        [jax.ShapeDtypeStruct((rows, cols), BF16)] * 2,
        [],
        5 * 10**8,
        10**6,
        [VMEM] * 4,
        [VMEM] * 2,
    )(up, down, got_up, got_down)


def partial_shapes(*shape):
    return [jax.ShapeDtypeStruct(shape, F32 if d == 0 else BF16) for d in range(4)]


def total(refs):
    t = refs[0][...]
    for r in refs[1:]:
        t = t + r[...].astype(F32)
    return t


def add_a(parts):
    def add_a_body(*refs):
        outs, t = refs[3:7], refs[7]
        x = place()["x"]
        t[...] = total(refs[0:3])
        for d in range(4):
            to = lax.rem(x + d, 4)
            rows, cols = pl.ds(mult(to // 2, 384), 384), pl.ds(mult(lax.rem(to, 2), BW), BW)
            outs[d][...] = t[rows, cols].astype(outs[d].dtype)

    return call(
        add_a_body,
        partial_shapes(384, 256),
        [pltpu.VMEM((768, 2 * BW), F32)],
        5 * 10**8,
        10**6,
        [VMEM] * 3,
        [VMEM] * 4,
    )(*parts)


def add_b(parts):
    def add_b_body(*refs):
        outs, t = refs[3:7], refs[7]
        z = place()["z"]
        t[...] = total(refs[0:3])
        for d in range(4):
            o = outs[d]
            o[...] = t[:, pl.ds(mult(lax.rem(z + d, 4), BW), BW)].astype(o.dtype)

    return call(
        add_b_body,
        partial_shapes(384, 256),
        [pltpu.VMEM((384, 4 * BW), F32)],
        5 * 10**8,
        10**6,
        [VMEM] * 3,
        [VMEM] * 4,
    )(*parts)


def finish(parts):
    def finish_body(*refs):
        qo, ko, vo = refs[8:]
        a = (total(refs[0:4]) * FACTOR).T
        b = (total(refs[4:8]) * FACTOR).T
        qo[:, 0:384] = a
        qo[:, 384:512] = b[:, 0:128]
        ko[...] = b[:, 128:256]
        vo[...] = b[:, 256:384]

    return call(
        finish_body,
        [
            jax.ShapeDtypeStruct((256, 512), F32),
            jax.ShapeDtypeStruct((256, 128), F32),
            jax.ShapeDtypeStruct((256, 128), F32),
        ],
        [],
        0,
        0,
        [VMEM] * 8,
        [VMEM] * 3,
    )(*parts)


def after(x, *deps):
    return lax.optimization_barrier((x, *deps))[0]


def ring(label, far, up, down, **axis):
    step = {k: -v for k, v in axis.items()}
    got_up = send(label + "_far_up", far[0], **axis)
    got_down = send(label + "_far_down", far[1], **step)
    ou, od = add_near(up, down, got_up, got_down)
    return send(label + "_up", ou, **axis), send(label + "_down", od, **step)


def per_device(hidden_in, queries, key_heads, saved_value_heads, out_grads, doc_ids):
    *kmsg, own = pack_keys(key_heads, saved_value_heads, doc_ids)
    q01, q02, q03, q11, q12, q13 = pack_queries(after(queries, own), out_grads)
    keys = [send("keys_y%d" % (d + 1), m, dy=d + 1) for d, m in enumerate(kmsg)]
    keep, give = pack_inputs(after(hidden_in, own))
    got = send("swap_inputs", give, dc=1)
    a1 = send("queries0_y1", q01, dy=1)
    a3 = send("queries0_y3", q03, dy=3)
    a2 = send("queries0_y2", q02, dy=2)
    before = send("half", jnp.concatenate([own] + keys, axis=0), dx=2)
    b1 = send("queries1_y1", after(q11, a1), dy=1)
    b3 = send("queries1_y3", after(q13, a1), dy=3)
    b2 = send("queries1_y2", after(q12, a1, a3), dy=2)
    sent = after(jnp.concatenate([keep, got], axis=0), a1, a2, a3)
    up = send("inputs_up", sent, dy=1)
    down = send("inputs_down", sent, dy=-1)

    def attend(h, dep, msgs):
        qs, gs = arrange(h, after(queries, *dep), out_grads, msgs)
        return attention(h, qs, gs, own, keys, before)

    dq0, dkv0, back0 = attend(0, (), (a1, a2, a3))
    swap0 = send("swap_dq0", dq0, dc=1)
    dq1, dkv1, back1 = attend(1, (dq0,), (b1, b2, b3))
    fwd = send("inputs_up2", after(up[0:128], dq1), dy=1)
    rev = send("inputs_down2", after(down[128:256], dq1), dy=-1)
    swap1 = send("swap_dq1", dq1, dc=1)
    ret = send("back", jnp.concatenate([back0, back1], axis=0), dx=2)
    ret = after(ret, fwd, rev, swap1).astype(F32)
    low = (jnp.concatenate([dkv0, dkv1], axis=0) + ret).astype(BF16)
    kv = (low, send("swap_dkv", low, dc=1))
    inputs = (sent, up, down, fwd, rev)
    gt = (dq0, swap0, dq1, swap1)

    ga = gather_a(gt)
    xs, *fa = far_a(ga, inputs)
    gb = gather_b(gt, kv)
    fb = far_b(after(gb, fa[0]), xs)
    ua, da, oa = near_a(after(ga, fb[0]), xs)
    ub, db, ob = near_b(after(gb, oa), xs)
    ra = ring("reduce_a", fa, ua, da, dz=1)
    rb = ring("reduce_b", fb, ub, db, dx=1)
    ma = add_a([oa, *ra])
    sa = [send("second_a_x%d" % d, ma[d], dx=d) for d in (1, 3, 2)]
    mb = add_b([ob, *rb])
    sb = [send("second_b_z%d" % d, mb[d], dz=d) for d in (1, 3, 2)]
    return finish([ma[0], *sa, mb[0], *sb])


def solution(mesh):
    return jax.shard_map(
        per_device,
        mesh=mesh,
        in_specs=(
            P("grp", "sp", None),
            P("grp", "sp", None),
            P("grp", "sp", None),
            P("grp", "sp", None),
            P("grp", "sp", None),
            P("grp", "sp"),
        ),
        out_specs=(P("grp", "sp"), P("grp", "sp"), P("grp", "sp")),
        check_vma=False,
    )
```

```python
import math

import jax
import jax.numpy as jnp
from jax import lax
from jax.experimental import pallas as pl
from jax.experimental.pallas import tpu as pltpu
from jax.sharding import PartitionSpec as P

HEAD = 128
NEG = -1e30
SCALE = 1.0 / math.sqrt(HEAD)
FACTOR = 16384 ** -0.5
BW = 256
VM = 32 * 1024 * 1024
BIG = 60 * 1024 * 1024
F32 = jnp.float32
BF16 = jnp.bfloat16
ANY = pl.BlockSpec(memory_space=pl.ANY)
VMEM = pl.BlockSpec(memory_space=pltpu.VMEM)


def place():
    g = lax.axis_index("grp")
    s = lax.axis_index("sp")
    return dict(
        z=g // 4, x=(s // 4) * 2 + (g // 2) % 2, c=lax.rem(g, 2), y=lax.rem(s, 4), xh=s // 4
    )


def pairs(dx=0, dy=0, dz=0, dc=0, only_half=None):
    out = []
    for z in range(4):
        for x in range(4):
            for y in range(4):
                for c in range(2):
                    if only_half is not None and x // 2 != only_half:
                        continue

                    def flat(z, x, y, c):
                        return (z * 4 + (x % 2) * 2 + c) * 8 + (x // 2) * 4 + y

                    out.append(
                        (
                            flat(z, x, y, c),
                            flat((z + dz) % 4, (x + dx) % 4, (y + dy) % 4, (c + dc) % 2),
                        )
                    )
    return out


def send(label, a, **k):
    with jax.named_scope(label):
        return lax.ppermute(a, ("grp", "sp"), pairs(**k))


def call(body, outs, scratch, flops, nbytes, in_specs, out_specs, vm=VM):
    return pl.pallas_call(
        body,
        name=body.__name__,
        out_shape=outs,
        in_specs=in_specs,
        out_specs=out_specs,
        scratch_shapes=scratch,
        compiler_params=pltpu.CompilerParams(vmem_limit_bytes=vm),
        cost_estimate=pl.CostEstimate(flops=flops, bytes_accessed=nbytes, transcendentals=0),
    )


def start_copies(todo, sems):
    made = [pltpu.make_async_copy(a, b, sems.at[i]) for i, (a, b) in enumerate(todo)]
    for m in made:
        m.start()
    return made


def run_copies(todo, sems):
    for m in start_copies(todo, sems):
        m.wait()


def mult(i, n):
    return pl.multiple_of(i * n, n)


def pack_keys(keys, values, ids):
    def pack_keys_body(k, v, i, k1, k2, k3, k0, sems):
        y = place()["y"]
        todo = []
        for d, o in ((1, k1), (3, k3), (2, k2), (0, k0)):
            for h in range(2):
                cols = pl.ds(mult(h * 4 + lax.rem(y + d, 4), 128), 128)
                todo += [
                    (k.at[0, :, cols], o.at[0:128, h * 256 : h * 256 + 128]),
                    (v.at[0, :, cols], o.at[0:128, h * 256 + 128 : h * 256 + 256]),
                ]
        made = start_copies(todo, sems)
        spread = jnp.broadcast_to(i[...].astype(F32), (16, 128)).astype(BF16)
        for o in (k1, k2, k3, k0):
            for part in range(4):
                o[128:144, part * 128 : (part + 1) * 128] = spread
        for m in made:
            m.wait()

    return call(
        pack_keys_body,
        [jax.ShapeDtypeStruct((144, 512), BF16)] * 4,
        [pltpu.SemaphoreType.DMA((16,))],
        10**8,
        10**6,
        [ANY] * 2 + [VMEM],
        [VMEM] * 4,
        BIG,
    )(keys, values, ids)


def pack_queries(queries, grads):
    def pack_queries_body(q, g, *refs):
        outs, sems = refs[:6], refs[6]
        y = place()["y"]
        todo = []
        for h in range(2):
            for d in (1, 2, 3):
                o = outs[h * 3 + d - 1]
                cols = pl.ds(mult(h * 4 + lax.rem(y + d, 4), 512), 512)
                todo += [(q.at[0, :, cols], o.at[:, 0:512]), (g.at[0, :, cols], o.at[:, 512:1024])]
        run_copies(todo, sems)

    return call(
        pack_queries_body,
        [jax.ShapeDtypeStruct((128, 1024), BF16)] * 6,
        [pltpu.SemaphoreType.DMA((12,))],
        10**8,
        10**6,
        [ANY] * 2,
        [VMEM] * 6,
        BIG,
    )(queries, grads)


def pack_inputs(hidden):
    def pack_inputs_body(x, keep, give, sems):
        c = place()["c"]
        todo = []
        for b in range(8):
            at = (b % 2) * 4 + b // 2
            for o, cc in ((keep, c), (give, 1 - c)):
                cols = pl.ds(mult(b * 2 + cc, BW), BW)
                todo.append((x.at[0, :, cols], o.at[:, at * BW : (at + 1) * BW]))
        run_copies(todo, sems)

    shape = jax.ShapeDtypeStruct((128, 8 * BW), BF16)
    return call(
        pack_inputs_body,
        [shape] * 2,
        [pltpu.SemaphoreType.DMA((16,))],
        10**9,
        10**6,
        [ANY],
        [VMEM] * 2,
        BIG,
    )(hidden)


def arrange(h, queries, grads, msgs):
    def arrange_body(q, g, q1, q2, q3, qs, gs, sems):
        y = place()["y"]
        cols, row = pl.ds(mult(h * 4 + y, 512), 512), pl.ds(mult(y, 128), 128)
        todo = [(q.at[0, :, cols], qs.at[row, :]), (g.at[0, :, cols], gs.at[row, :])]
        for d, m in ((1, q1), (2, q2), (3, q3)):
            row = pl.ds(mult(lax.rem(y - d + 4, 4), 128), 128)
            todo += [(m.at[:, 0:512], qs.at[row, :]), (m.at[:, 512:1024], gs.at[row, :])]
        run_copies(todo, sems)

    return call(
        arrange_body,
        [jax.ShapeDtypeStruct((512, 512), BF16)] * 2,
        [pltpu.SemaphoreType.DMA((8,))],
        6 * 10**9,
        10**6,
        [ANY] * 5,
        [VMEM] * 2,
    )(queries, grads, *msgs)


def attention(h, queries, grads, own, keys, before):
    def attention_body(qs, gs, kv, k1, k2, k3, pv, dq, dkv, dprev, ks, vs, ids, bias, acck, accv, sems):
        here = place()
        y, xh = here["y"], here["xh"]
        todo = []
        for d, k in ((0, kv), (1, k1), (2, k2), (3, k3)):
            r = mult(lax.rem(y - d + 4, 4), 128)
            todo += [
                (k.at[0:128, h * 256 : h * 256 + 128], ks.at[pl.ds(r + 512, 128), :]),
                (k.at[0:128, h * 256 + 128 : h * 256 + 256], vs.at[pl.ds(r + 512, 128), :]),
                (k.at[128:144, 0:128], ids.at[d * 16 + 64 : d * 16 + 80, :]),
            ]
            lo = d * 144
            todo += [
                (pv.at[lo : lo + 128, h * 256 : h * 256 + 128], ks.at[pl.ds(r, 128), :]),
                (pv.at[lo : lo + 128, h * 256 + 128 : h * 256 + 256], vs.at[pl.ds(r, 128), :]),
                (pv.at[lo + 128 : lo + 144, 0:128], ids.at[d * 16 : d * 16 + 16, :]),
            ]
        run_copies(todo, sems)

        low = xh * 512
        own_ids = ids[64:128, :].astype(F32)
        prev_ids = ids[0:64, :].astype(F32)
        second = xh.astype(F32)

        def count(top):
            a = jnp.where(own_ids <= top, 1.0, 0.0)
            b = jnp.where(prev_ids <= top, 1.0, 0.0)
            each = jnp.sum(a + second * b, axis=1, keepdims=True)
            return (jnp.sum(each, axis=0, keepdims=True) * (1.0 / 16)).astype(jnp.int32)

        first, both = count(0.5), count(1.5)
        acck[...] = jnp.zeros_like(acck)
        accv[...] = jnp.zeros_like(accv)
        for blk in range(2):
            lo = blk * 256
            t = lax.broadcasted_iota(jnp.int32, (1, 256), 1) + lo
            ta = t + low
            start = jnp.where(ta < first, 0, jnp.where(ta < both, first, both)) - low
            u = lax.broadcasted_iota(jnp.int32, (768, 256), 0) + (lo - 512)
            bias[blk] = jnp.where((u <= t) & (u >= start), 0.0, NEG)

        def head(hq, _):
            cols = pl.ds(mult(hq, 128), 128)
            for blk in range(2):
                lo = blk * 256
                keys = ks[lo : lo + 768, :]
                vals = vs[lo : lo + 768, :]
                qq = qs[lo : lo + 256, cols]
                gg = gs[lo : lo + 256, cols]
                nt = (((1,), (1,)), ((), ()))
                sc = lax.dot_general(keys, qq, nt, preferred_element_type=F32) * SCALE + bias[blk]
                e = jnp.exp(sc - jnp.max(sc, axis=0, keepdims=True))
                p = e * (1.0 / jnp.sum(e, axis=0, keepdims=True))
                p_low = p.astype(BF16)
                dp = lax.dot_general(vals, gg, nt, preferred_element_type=F32)
                delta = jnp.sum(p_low.astype(F32) * dp, axis=0, keepdims=True)
                ds = (p * (dp - delta) * SCALE).astype(BF16)
                tn = (((0,), (0,)), ((), ()))
                dqt = lax.dot_general(keys, ds, tn, preferred_element_type=F32)
                dq[cols, lo : lo + 256] = dqt.astype(BF16)
                acck[lo : lo + 768, :] += jnp.dot(ds, qq, preferred_element_type=F32)
                accv[lo : lo + 768, :] += jnp.dot(p_low, gg, preferred_element_type=F32)
            return 0

        lax.fori_loop(0, 4, head, 0, unroll=4)
        dkv[0:128, :] = acck[512:1024, :].T
        dkv[128:256, :] = accv[512:1024, :].T
        dprev[0:128, :] = acck[0:512, :].astype(BF16).T
        dprev[128:256, :] = accv[0:512, :].astype(BF16).T

    return call(
        attention_body,
        [
            jax.ShapeDtypeStruct((512, 512), BF16),
            jax.ShapeDtypeStruct((256, 512), F32),
            jax.ShapeDtypeStruct((256, 512), BF16),
        ],
        [
            pltpu.VMEM((1024, 128), BF16),
            pltpu.VMEM((1024, 128), BF16),
            pltpu.VMEM((128, 128), BF16),
            pltpu.VMEM((2, 768, 256), F32),
            pltpu.VMEM((1024, 128), F32),
            pltpu.VMEM((1024, 128), F32),
            pltpu.SemaphoreType.DMA((32,)),
        ],
        12 * 10**9,
        10**6,
        [VMEM] * 2 + [ANY] * 5,
        [VMEM] * 3,
    )(queries, grads, own, *keys, before)


def gather_a(gt):
    def gather_a_body(a0, b0, a1, b1, ga, sems):
        todo = []
        for h, pair in enumerate(((a0, b0), (a1, b1))):
            for i, src in enumerate(pair):
                to = ga.at[h * 384 : (h + 1) * 384, i * 512 : (i + 1) * 512]
                todo.append((src.at[0:384, :], to))
        run_copies(todo, sems)

    return call(
        gather_a_body,
        jax.ShapeDtypeStruct((768, 1024), BF16),
        [pltpu.SemaphoreType.DMA((4,))],
        10**8,
        10**6,
        [ANY] * 4,
        VMEM,
    )(*gt)


def gather_b(gt, kv):
    def gather_b_body(a0, b0, a1, b1, k, l, gb, sems):
        todo = []
        for h, pair in enumerate(((a0, b0), (a1, b1))):
            for i, (src, low) in enumerate(zip(pair, (k, l))):
                cols = slice(i * 512, (i + 1) * 512)
                todo += [
                    (src.at[384:512, :], gb.at[h * 384 : h * 384 + 128, cols]),
                    (low.at[h * 256 : (h + 1) * 256, :], gb.at[h * 384 + 128 : (h + 1) * 384, cols]),
                ]
        run_copies(todo, sems)

    return call(
        gather_b_body,
        jax.ShapeDtypeStruct((768, 1024), BF16),
        [pltpu.SemaphoreType.DMA((8,))],
        10**8,
        10**6,
        [ANY] * 6,
        VMEM,
    )(*gt, *kv)


def product(a, b):
    return jnp.dot(a, b, preferred_element_type=F32)


def z_cols(xs, z):
    return jnp.concatenate(
        [xs[:, pl.ds(mult(z, BW), BW)], xs[:, pl.ds(mult(z + 4, BW), BW)]], axis=1
    )


def far_a(ga, inputs):
    def far_a_body(g, own, r1, r3, r2a, r2b, xs, up, down, sems):
        here = place()
        y = here["y"]

        def at(d, half):
            row = lax.rem(y - d + 4, 4) * 128 + half * 512
            return xs.at[pl.ds(pl.multiple_of(row, 128), 128), :]

        todo = []
        for d, r in ((0, own), (1, r1), (3, r3)):
            todo += [(r.at[0:128, :], at(d, 0)), (r.at[128:256, :], at(d, 1))]
        run_copies(todo + [(r2a, at(2, 0)), (r2b, at(2, 1))], sems)
        p = product(g[...], z_cols(xs, lax.rem(here["z"] + 2, 4)))
        up[...] = p[:, 0:BW].astype(BF16)
        down[...] = p[:, BW:].astype(BF16)

    return call(
        far_a_body,
        [jax.ShapeDtypeStruct((1024, 8 * BW), BF16)] + [jax.ShapeDtypeStruct((768, BW), BF16)] * 2,
        [pltpu.SemaphoreType.DMA((8,))],
        10**9,
        10**6,
        [VMEM] + [ANY] * 5,
        [VMEM] * 3,
    )(ga, *inputs)


def x_product(g, xs, to, lo, size):
    cols = xs[:, pl.ds(mult(lax.rem(to, 2) * 4 + lo, BW), size * BW)]
    return product(g[pl.ds(mult(to // 2, 384), 384), :], cols)


def far_b(gb, xs):
    def far_b_body(g, x, up, down):
        to = lax.rem(place()["x"] + 2, 4)
        for o, lo in ((up, 0), (down, 2)):
            o[...] = x_product(g, x, to, lo, 2).astype(BF16)

    return call(
        far_b_body,
        [jax.ShapeDtypeStruct((384, 2 * BW), BF16)] * 2,
        [],
        10**9,
        10**6,
        [VMEM] * 2,
        [VMEM] * 2,
    )(gb, xs)


def near_a(ga, xs):
    def near_a_body(g, x, up, down, own):
        z = place()["z"]
        for o, d in ((up, 1), (down, 3), (own, 0)):
            o[...] = product(g[...], z_cols(x, lax.rem(z + d, 4)))

    return call(
        near_a_body,
        [jax.ShapeDtypeStruct((768, 2 * BW), F32)] * 3,
        [],
        10**9,
        10**6,
        [VMEM] * 2,
        [VMEM] * 3,
    )(ga, xs)


def near_b(gb, xs):
    def near_b_body(g, x, up, down, own):
        for o, d in ((up, 1), (down, 3), (own, 0)):
            o[...] = x_product(g, x, lax.rem(place()["x"] + d, 4), 0, 4)

    return call(
        near_b_body,
        [jax.ShapeDtypeStruct((384, 4 * BW), F32)] * 3,
        [],
        10**9,
        10**6,
        [VMEM] * 2,
        [VMEM] * 3,
    )(gb, xs)


def add_near(up, down, got_up, got_down):
    rows, cols = up.shape
    half = cols // 2

    def add_near_body(u, d, gu, gd, ou, od):
        ou[:, 0:half] = (u[:, 0:half] + gu[...].astype(F32)).astype(BF16)
        ou[:, half:] = u[:, half:].astype(BF16)
        od[:, 0:half] = d[:, 0:half].astype(BF16)
        od[:, half:] = (d[:, half:] + gd[...].astype(F32)).astype(BF16)

    return call(
        add_near_body,
        [jax.ShapeDtypeStruct((rows, cols), BF16)] * 2,
        [],
        5 * 10**8,
        10**6,
        [VMEM] * 4,
        [VMEM] * 2,
    )(up, down, got_up, got_down)


def partial_shapes(*shape):
    return [jax.ShapeDtypeStruct(shape, F32 if d == 0 else BF16) for d in range(4)]


def total(refs):
    t = refs[0][...]
    for r in refs[1:]:
        t = t + r[...].astype(F32)
    return t


def add_a(parts):
    def add_a_body(*refs):
        outs, t = refs[3:7], refs[7]
        x = place()["x"]
        t[...] = total(refs[0:3])
        for d in range(4):
            to = lax.rem(x + d, 4)
            rows, cols = pl.ds(mult(to // 2, 384), 384), pl.ds(mult(lax.rem(to, 2), BW), BW)
            outs[d][...] = t[rows, cols].astype(outs[d].dtype)

    return call(
        add_a_body,
        partial_shapes(384, 256),
        [pltpu.VMEM((768, 2 * BW), F32)],
        5 * 10**8,
        10**6,
        [VMEM] * 3,
        [VMEM] * 4,
    )(*parts)


def add_b(parts):
    def add_b_body(*refs):
        outs, t = refs[3:7], refs[7]
        z = place()["z"]
        t[...] = total(refs[0:3])
        for d in range(4):
            o = outs[d]
            o[...] = t[:, pl.ds(mult(lax.rem(z + d, 4), BW), BW)].astype(o.dtype)

    return call(
        add_b_body,
        partial_shapes(384, 256),
        [pltpu.VMEM((384, 4 * BW), F32)],
        5 * 10**8,
        10**6,
        [VMEM] * 3,
        [VMEM] * 4,
    )(*parts)


def finish(parts):
    def finish_body(*refs):
        qo, ko, vo = refs[8:]
        a = (total(refs[0:4]) * FACTOR).T
        b = (total(refs[4:8]) * FACTOR).T
        qo[:, 0:384] = a
        qo[:, 384:512] = b[:, 0:128]
        ko[...] = b[:, 128:256]
        vo[...] = b[:, 256:384]

    return call(
        finish_body,
        [
            jax.ShapeDtypeStruct((256, 512), F32),
            jax.ShapeDtypeStruct((256, 128), F32),
            jax.ShapeDtypeStruct((256, 128), F32),
        ],
        [],
        0,
        0,
        [VMEM] * 8,
        [VMEM] * 3,
    )(*parts)


def after(x, *deps):
    return lax.optimization_barrier((x, *deps))[0]


def ring(label, far, up, down, **axis):
    step = {k: -v for k, v in axis.items()}
    got_up = send(label + "_far_up", far[0], **axis)
    got_down = send(label + "_far_down", far[1], **step)
    ou, od = add_near(up, down, got_up, got_down)
    return send(label + "_up", ou, **axis), send(label + "_down", od, **step)


def per_device(hidden_in, queries, key_heads, saved_value_heads, out_grads, doc_ids):
    *kmsg, own = pack_keys(key_heads, saved_value_heads, doc_ids)
    q01, q02, q03, q11, q12, q13 = pack_queries(after(queries, own), out_grads)
    keys = [send("keys_y%d" % (d + 1), m, dy=d + 1) for d, m in enumerate(kmsg)]
    keep, give = pack_inputs(after(hidden_in, own))
    got = send("swap_inputs", give, dc=1)
    a1 = send("queries0_y1", q01, dy=1)
    a3 = send("queries0_y3", q03, dy=3)
    a2 = send("queries0_y2", q02, dy=2)
    before = send("half", jnp.concatenate([own] + keys, axis=0), dx=2)
    b1 = send("queries1_y1", q11, dy=1)
    b3 = send("queries1_y3", q13, dy=3)
    b2 = send("queries1_y2", q12, dy=2)
    sent = after(jnp.concatenate([keep, got], axis=0), a1, a2, a3)
    up = send("inputs_up", sent, dy=1)
    down = send("inputs_down", sent, dy=-1)

    def attend(h, dep, msgs):
        qs, gs = arrange(h, after(queries, *dep), out_grads, msgs)
        return attention(h, qs, gs, own, keys, before)

    dq0, dkv0, back0 = attend(0, (), (a1, a2, a3))
    swap0 = send("swap_dq0", dq0, dc=1)
    dq1, dkv1, back1 = attend(1, (dq0,), (b1, b2, b3))
    fwd = send("inputs_up2", after(up[0:128], dq1), dy=1)
    rev = send("inputs_down2", after(down[128:256], dq1), dy=-1)
    swap1 = send("swap_dq1", dq1, dc=1)
    ret = send("back", jnp.concatenate([back0, back1], axis=0), dx=2)
    ret = after(ret, fwd, rev, swap1).astype(F32)
    low = (jnp.concatenate([dkv0, dkv1], axis=0) + ret).astype(BF16)
    kv = (low, send("swap_dkv", low, dc=1))
    inputs = (sent, up, down, fwd, rev)
    gt = (dq0, swap0, dq1, swap1)

    ga = gather_a(gt)
    xs, *fa = far_a(ga, inputs)
    gb = gather_b(gt, kv)
    fb = far_b(after(gb, fa[0]), xs)
    ua, da, oa = near_a(after(ga, fb[0]), xs)
    ub, db, ob = near_b(after(gb, oa), xs)
    ra = ring("reduce_a", fa, ua, da, dz=1)
    rb = ring("reduce_b", fb, ub, db, dx=1)
    ma = add_a([oa, *ra])
    sa = [send("second_a_x%d" % d, ma[d], dx=d) for d in (1, 3, 2)]
    mb = add_b([ob, *rb])
    sb = [send("second_b_z%d" % d, mb[d], dz=d) for d in (1, 3, 2)]
    return finish([ma[0], *sa, mb[0], *sb])


def solution(mesh):
    return jax.shard_map(
        per_device,
        mesh=mesh,
        in_specs=(
            P("grp", "sp", None),
            P("grp", "sp", None),
            P("grp", "sp", None),
            P("grp", "sp", None),
            P("grp", "sp", None),
            P("grp", "sp"),
        ),
        out_specs=(P("grp", "sp"), P("grp", "sp"), P("grp", "sp")),
        check_vma=False,
    )
```
